32 devices in a mesh: lon: 16 (over z, x, core), lat: 2 (over y).
Axes of the slice: x: 2, y: 2, z: 4, core: 2. Of those that a mesh axis runs over, the one named last changes fastest.
Arguments:
- inputs: bfloat16 [96, 768, 128], P('lat', 'lon'), may hold values from -6 to 6
- weight: bfloat16 [3, 3, 128, 128], replicated, may hold values from -0.1875 to 0.1875
- bias: float32 [128], replicated, may hold values from -3 to 3
- cotangent: bfloat16 [96, 768, 128], P('lat', 'lon'), may hold values from -6 to 6
Outputs:
- outputs: bfloat16 [96, 768, 128], P('lat', 'lon')
- input_grad: bfloat16 [96, 768, 128], P('lat', 'lon')
- weight_grad: float32 [3, 3, 128, 128], replicated
- bias_grad: float32 [128], replicated
The draws below stay inside these ranges and needn't reach their ends.
All inputs are finite; a program needn't handle non-finite values.
Results may differ from the reference program's by a relative error of at most 0.006.
Values may be sent and summed in bfloat16 or wider, within the bound.
A program may use at most 64 MiB of HBM per device.

```python
import jax
import jax.numpy as jnp
from jax import lax

C = 128
NLAT = 96
NLON = 768


def block_scale(rng, shape, split, low, high):
    def one(axis_at, parts):
        draws = jax.random.uniform(jax.random.fold_in(jax.random.fold_in(rng, 6), axis_at), (parts,), jnp.float32, low / len(split), high / len(split))
        return jnp.repeat(jnp.exp(draws), shape[axis_at] // parts).reshape((-1,) + (1,) * (len(shape) - axis_at - 1))

    level = one(*split[0])
    for cut in split[1:]:
        level = level * one(*cut)
    return level


def normal_values(stream_key, extent, deviation, most, cuts=(), kind=jnp.bfloat16):
    gain = block_scale(stream_key, extent, cuts, -0.22, 0.18) if cuts else 1.0
    entries = jax.random.normal(stream_key, extent, jnp.float32) * deviation * gain
    return jnp.minimum(jnp.maximum(entries, -most), most).astype(kind)


def setup_inputs(seed: int = 0) -> dict:
    arg_keys = jax.random.split(jax.random.key(seed), 5)
    inputs = normal_values(arg_keys[0], (NLAT, NLON, C), 1.0, 6.0, ((0, 2), (1, 16)))
    weight = normal_values(arg_keys[1], (3, 3, C, C), (9 * C) ** -0.5, 0.1875)
    bias = normal_values(arg_keys[2], (C,), 0.5, 3.0, (), jnp.float32)
    cotangent = normal_values(arg_keys[3], (NLAT, NLON, C), 1.0, 6.0, ((0, 2), (1, 16)))
    return dict(inputs=inputs, weight=weight, bias=bias, cotangent=cotangent)


def pad_field(field):
    half = field.shape[1] // 2
    wide = jnp.concatenate([field[:, -1:], field, field[:, :1]], axis=1)
    top = jnp.roll(field[0], -half, axis=0)
    bottom = jnp.roll(field[-1], -half, axis=0)
    top_wide = jnp.concatenate([top[-1:], top, top[:1]], axis=0)
    bottom_wide = jnp.concatenate([bottom[-1:], bottom, bottom[:1]], axis=0)
    return jnp.concatenate([top_wide[None], wide, bottom_wide[None]], axis=0)

def reference(inputs, weight, bias, cotangent):
    rows, cols, chans = inputs.shape
    padded = pad_field(inputs)
    pre = jnp.zeros((rows * cols, chans), jnp.float32) + bias[None, :]
    for tap_a in range(3):
        for tap_b in range(3):
            window = padded[tap_a:tap_a + rows, tap_b:tap_b + cols].reshape(rows * cols, chans)
            pre = pre + jnp.dot(window, weight[tap_a, tap_b], preferred_element_type=jnp.float32)
    sig = jax.nn.sigmoid(pre)
    outputs = (pre * sig).astype(jnp.bfloat16).reshape(rows, cols, chans)
    flat_cot = cotangent.reshape(rows * cols, chans).astype(jnp.float32)
    pre_grad = (flat_cot * sig * (1.0 + pre * (1.0 - sig))).astype(jnp.bfloat16)
    padded_grad = jnp.zeros((rows + 2, cols + 2, chans), jnp.float32)
    scale = 1.0 / jnp.sqrt(jnp.float32(rows * cols))
    taps = []
    for tap_a in range(3):
        for tap_b in range(3):
            back = jnp.dot(pre_grad, weight[tap_a, tap_b].T, preferred_element_type=jnp.float32)
            padded_grad = padded_grad.at[tap_a:tap_a + rows, tap_b:tap_b + cols].add(back.reshape(rows, cols, chans))
            window = padded[tap_a:tap_a + rows, tap_b:tap_b + cols].reshape(rows * cols, chans)
            taps.append(lax.dot_general(window, pre_grad, (((0,), (0,)), ((), ())), preferred_element_type=jnp.float32))
    weight_grad = jnp.stack(taps).reshape(3, 3, chans, chans) * scale
    bias_grad = lax.optimization_barrier(jnp.sum(pre_grad.astype(jnp.float32), axis=0)) * scale
    unused, pull = jax.vjp(pad_field, inputs.astype(jnp.float32))
    input_grad = pull(padded_grad)[0].astype(jnp.bfloat16)
    return (outputs, input_grad, weight_grad, bias_grad)
```

```python
import functools
import math

import jax
import jax.numpy as jnp
from jax import lax
from jax.experimental import pallas as pl
from jax.experimental.pallas import tpu as pltpu
from jax.sharding import PartitionSpec as P

MESH = pl.DeviceIdType.MESH
F32 = jnp.float32
BF16 = jnp.bfloat16
CHUNK = 8
EXTRA = 16


def kernel(
    lons, lats, x_ref, w_ref, b_ref, c_ref,
    out_ref, gin_ref, wg_ref, bg_ref,
    xc, pc, pg, hrows, hcols, hcorn, hc32, scol32, scol, dwt, bacc,
    sbuf, r1, s2, r2, gath,
    ssem, rsem, s1sem, r1sem, s2sem, r2sem, s3sem, r3sem,
):
    rows, cols, ch = x_ref.shape
    lon, lat = lax.axis_index("lon"), lax.axis_index("lat")
    half = lons // 2
    gl, gt = math.gcd(lons, 4), math.gcd(lats, 2)
    n1 = gl * gt
    n2 = (lons // gl) * (lats // gt)
    part = 9 * ch // n1

    top, bottom = lat == 0, lat == lats - 1
    n_lat = jnp.where(top, lat, lat - 1)
    s_lat = jnp.where(bottom, lat, lat + 1)
    n_lon = jnp.where(top, lon + half, lon)
    s_lon = jnp.where(bottom, lon + half, lon)

    def at(lon_at, lat_at):
        return (lax.rem(lon_at + lons, lons), lat_at)

    north, south = at(n_lon, n_lat), at(s_lon, s_lat)
    west, east = at(lon - 1, lat), at(lon + 1, lat)
    nw, ne = at(n_lon - 1, n_lat), at(n_lon + 1, n_lat)
    sw, se = at(s_lon - 1, s_lat), at(s_lon + 1, s_lat)

    g1 = lax.rem(lon, gl) * gt + lax.rem(lat, gt)
    g2 = (lon // gl) * (lats // gt) + lat // gt

    def peer1(k):
        q = lax.rem(g1 + k, n1)
        return q, ((lon // gl) * gl + q // gt, (lat // gt) * gt + lax.rem(q, gt))

    def peer2(k):
        q = lax.rem(g2 + k, n2)
        wide = lats // gt
        return q, ((q // wide) * gl + lax.rem(lon, gl), lax.rem(q, wide) * gt + lax.rem(lat, gt))

    barrier = pltpu.get_barrier_semaphore()
    greeted = [north, south, west, east, nw, ne, sw, se]
    greeted += [peer1(k)[1] for k in range(1, n1)] + [peer2(k)[1] for k in range(1, n2)]
    for device in greeted:
        pl.semaphore_signal(barrier, inc=1, device_id=device, device_id_type=MESH)

    def stage_columns(turn, src):
        def body(i, carry):
            for k in range(4):
                r = i * 4 + k
                scol32[0, pl.ds(r, 1), :] = src[r, 0:16, :].astype(F32)[0:1]
                scol32[1, pl.ds(r, 1), :] = src[r, cols - 16 : cols, :].astype(F32)[15:16]
            return carry

        lax.fori_loop(0, rows // 4, body, 0)
        scol[turn] = scol32[...].astype(BF16)

    def halo_copies(turn, src):
        lo, hi = slice(0, 16), slice(cols - 16, cols)
        to_north = jnp.where(top, 0, 1)
        to_south = jnp.where(bottom, 1, 0)
        to_nw, to_ne = jnp.where(top, 1, 3), jnp.where(top, 0, 2)
        to_sw, to_se = jnp.where(bottom, 3, 1), jnp.where(bottom, 2, 0)
        plan = [
            (scol.at[turn, 1], hcols.at[turn, 0], 2, east),
            (scol.at[turn, 0], hcols.at[turn, 1], 3, west),
            (src.at[0], hrows.at[turn, to_north], to_north, north),
            (src.at[rows - 1], hrows.at[turn, to_south], to_south, south),
            (src.at[0, lo, :], hcorn.at[turn, to_nw], 4 + to_nw, nw),
            (src.at[0, hi, :], hcorn.at[turn, to_ne], 4 + to_ne, ne),
            (src.at[rows - 1, lo, :], hcorn.at[turn, to_sw], 4 + to_sw, sw),
            (src.at[rows - 1, hi, :], hcorn.at[turn, to_se], 4 + to_se, se),
        ]
        return [
            pltpu.make_async_remote_copy(
                src_ref=s, dst_ref=d, send_sem=ssem.at[turn, i], recv_sem=rsem.at[turn, sem],
                device_id=device, device_id_type=MESH,
            )
            for i, (s, d, sem, device) in enumerate(plan)
        ]

    def halo_wait(turn):
        slots = [hrows.at[turn, 0], hrows.at[turn, 1], hcols.at[turn, 0], hcols.at[turn, 1]]
        slots += [hcorn.at[turn, i] for i in range(4)]
        for i, slot in enumerate(slots):
            pltpu.make_async_remote_copy(
                src_ref=slot, dst_ref=slot, send_sem=ssem.at[turn, i], recv_sem=rsem.at[turn, i],
                device_id=east, device_id_type=MESH,
            ).wait_recv()

    place = lax.broadcasted_iota(jnp.int32, (cols, ch), 0)

    def put_row(dst, at_row, centre, west_cell, east_cell):
        wide = centre.astype(F32)
        before = jnp.where(place == 0, west_cell, pltpu.roll(wide, 1, 0))
        after = jnp.where(place == cols - 1, east_cell, pltpu.roll(wide, cols - 1, 0))
        dst[at_row, :, 0:ch] = before.astype(BF16)
        dst[at_row, :, ch : 2 * ch] = centre
        dst[at_row, :, 2 * ch : 3 * ch] = after.astype(BF16)

    def widen(turn, src, dst):
        hc32[...] = hcols[turn].astype(F32)

        def body(i, carry):
            for k in range(4):
                r = i * 4 + k
                put_row(dst, r + 1, src[r], hc32[0, pl.ds(r, 1), :], hc32[1, pl.ds(r, 1), :])
            return carry

        lax.fori_loop(0, rows // 4, body, 0)
        for side, at_row in ((0, 0), (1, rows + 1)):
            west_cell = hcorn[turn, 2 * side].astype(F32)[15:16]
            east_cell = hcorn[turn, 2 * side + 1].astype(F32)[0:1]
            put_row(dst, at_row, hrows[turn, side], west_cell, east_cell)

    def windows(src, r0):
        return jnp.concatenate(
            [src[pl.ds(r0 + a, CHUNK)].reshape(CHUNK * cols, 3 * ch) for a in range(3)], axis=1
        )

    stage_columns(0, x_ref)
    pl.semaphore_wait(barrier, len(greeted))
    first = halo_copies(0, x_ref)
    for copy in first:
        copy.start()
    dwt[...] = jnp.zeros_like(dwt)
    bacc[...] = jnp.zeros_like(bacc)
    halo_wait(0)
    widen(0, x_ref, xc)

    def forward(i, carry):
        r0 = i * CHUNK
        lhs = windows(xc, r0)
        weight = w_ref[...].reshape(9 * ch, ch)
        pre = jnp.dot(lhs, weight, preferred_element_type=F32) + b_ref[...]
        sig = 1.0 / (1.0 + jnp.exp(-pre))
        out_ref[pl.ds(r0, CHUNK)] = (pre * sig).astype(BF16).reshape(CHUNK, cols, ch)
        cot = c_ref[pl.ds(r0, CHUNK)].reshape(CHUNK * cols, ch).astype(F32)
        grad = (cot * sig * (1.0 + pre * (1.0 - sig))).astype(BF16)
        pg[pl.ds(r0, CHUNK)] = grad.reshape(CHUNK, cols, ch)
        bacc[...] += jnp.sum(grad.astype(F32), axis=0, keepdims=True)
        dwt[...] += lax.dot_general(grad, lhs, (((0,), (0,)), ((), ())), preferred_element_type=F32)
        return carry

    lax.fori_loop(0, rows // CHUNK, forward, 0)

    stage_columns(1, pg)
    second = halo_copies(1, pg)
    for copy in second:
        copy.start()

    line = lax.broadcasted_iota(jnp.int32, (EXTRA, ch), 0)

    def split(total):
        first_part = total.astype(BF16).astype(F32)
        rest = total - first_part
        second_part = rest.astype(BF16).astype(F32)
        third = rest - second_part
        rows_of = jnp.where(line == 0, first_part, jnp.where(line == 1, second_part, jnp.where(line == 2, third, 0.0)))
        return rows_of.astype(BF16)

    for tap in range(9):
        block = dwt[:, tap * ch : (tap + 1) * ch].T.astype(BF16)
        low = tap * ch
        while low < (tap + 1) * ch:
            q = low // part
            high = min((tap + 1) * ch, (q + 1) * part)
            sbuf[q, low - q * part : high - q * part, :] = block[low - tap * ch : high - tap * ch]
            low = high
    bias_rows = split(bacc[...])
    for q in range(n1):
        sbuf[q, part : part + EXTRA, :] = bias_rows

    def copies1():
        result = []
        for k in range(1, n1):
            q, device = peer1(k)
            result.append(
                pltpu.make_async_remote_copy(
                    src_ref=sbuf.at[q], dst_ref=r1.at[g1], send_sem=s1sem.at[k], recv_sem=r1sem.at[g1],
                    device_id=device, device_id_type=MESH,
                )
            )
        return result

    def wait_from(buffer, sems, send_sems, k, q):
        pltpu.make_async_remote_copy(
            src_ref=buffer.at[q], dst_ref=buffer.at[q], send_sem=send_sems.at[k], recv_sem=sems.at[q],
            device_id=east, device_id_type=MESH,
        ).wait_recv()

    sent1 = copies1()
    for copy in sent1:
        copy.start()
    r1[g1] = sbuf[g1]

    halo_wait(1)
    widen(1, pg, pc)

    def kernel_for(taps):
        return jnp.concatenate([w_ref[a, b] for a in taps for b in (2, 1, 0)], axis=1)

    def back(lhs, rhs):
        return lax.dot_general(lhs, rhs, (((1,), (1,)), ((), ())), preferred_element_type=F32)

    def backward(i, carry):
        r0 = i * CHUNK
        grad = back(windows(pc, r0), kernel_for((2, 1, 0)))
        gin_ref[pl.ds(r0, CHUNK)] = grad.astype(BF16).reshape(CHUNK, cols, ch)
        return carry

    lax.fori_loop(0, rows // CHUNK, backward, 0)

    plain = kernel_for((2, 1, 0))
    lhs = jnp.concatenate([pc[a] for a in range(3)], axis=1)
    gin_ref[0] = back(lhs, jnp.where(top, kernel_for((0, 1, 0)), plain)).astype(BF16)
    lhs = jnp.concatenate([pc[rows - 1 + a] for a in range(3)], axis=1)
    gin_ref[rows - 1] = back(lhs, jnp.where(bottom, kernel_for((2, 1, 2)), plain)).astype(BF16)

    for k in range(1, n1):
        wait_from(r1, r1sem, s1sem, k, peer1(k)[0])

    def added(buffer, count):
        total = buffer[0].astype(F32)
        for q in range(1, count):
            total = total + buffer[q].astype(F32)
        return total[:part], jnp.sum(total[part:], axis=0, keepdims=True)

    block, bias_sum = added(r1, n1)
    s2[0:part, :] = block.astype(BF16)
    s2[part : part + EXTRA, :] = split(bias_sum)
    sent2 = []
    for k in range(1, n2):
        q, device = peer2(k)
        sent2.append(
            pltpu.make_async_remote_copy(
                src_ref=s2, dst_ref=r2.at[g2], send_sem=s2sem.at[k], recv_sem=r2sem.at[g2],
                device_id=device, device_id_type=MESH,
            )
        )
    for copy in sent2:
        copy.start()
    r2[g2] = s2[...]
    for k in range(1, n2):
        wait_from(r2, r2sem, s2sem, k, peer2(k)[0])
    block, bias_sum = added(r2, n2)
    scale = 1.0 / math.sqrt(rows * cols * lons * lats)
    bg_ref[...] = bias_sum * scale
    gath[g1] = (block * scale).astype(BF16)
    sent3 = []
    for k in range(1, n1):
        q, device = peer1(k)
        sent3.append(
            pltpu.make_async_remote_copy(
                src_ref=gath.at[g1], dst_ref=gath.at[g1], send_sem=s3sem.at[k], recv_sem=r3sem.at[g1],
                device_id=device, device_id_type=MESH,
            )
        )
    for copy in sent3:
        copy.start()
    for k in range(1, n1):
        wait_from(gath, r3sem, s3sem, k, peer1(k)[0])
    for q in range(n1):
        wg_ref[q] = gath[q].astype(F32)
    for copy in first + second + sent1 + sent2 + sent3:
        copy.wait_send()


def shards(lons, lats, inputs, weight, bias, cotangent):
    rows, cols, ch = inputs.shape
    gl, gt = math.gcd(lons, 4), math.gcd(lats, 2)
    n1 = gl * gt
    n2 = (lons // gl) * (lats // gt)
    part = 9 * ch // n1
    vmem = pl.BlockSpec(memory_space=pltpu.VMEM)
    dma = pltpu.SemaphoreType.DMA
    outputs, input_grad, weight_grad, bias_grad = pl.pallas_call(
        functools.partial(kernel, lons, lats),
        out_shape=(
            jax.ShapeDtypeStruct((rows, cols, ch), BF16),
            jax.ShapeDtypeStruct((rows, cols, ch), BF16),
            jax.ShapeDtypeStruct((n1, part, ch), F32),
            jax.ShapeDtypeStruct((1, ch), F32),
        ),
        in_specs=[vmem] * 4,
        out_specs=(vmem,) * 4,
        scratch_shapes=[
            pltpu.VMEM((rows + 2, cols, 3 * ch), BF16),
            pltpu.VMEM((rows + 2, cols, 3 * ch), BF16),
            pltpu.VMEM((rows, cols, ch), BF16),
            pltpu.VMEM((2, 2, cols, ch), BF16),
            pltpu.VMEM((2, 2, rows, ch), BF16),
            pltpu.VMEM((2, 4, 16, ch), BF16),
            pltpu.VMEM((2, rows, ch), F32),
            pltpu.VMEM((2, rows, ch), F32),
            pltpu.VMEM((2, 2, rows, ch), BF16),
            pltpu.VMEM((ch, 9 * ch), F32),
            pltpu.VMEM((1, ch), F32),
            pltpu.VMEM((n1, part + EXTRA, ch), BF16),
            pltpu.VMEM((n1, part + EXTRA, ch), BF16),
            pltpu.VMEM((part + EXTRA, ch), BF16),
            pltpu.VMEM((n2, part + EXTRA, ch), BF16),
            pltpu.VMEM((n1, part, ch), BF16),
            dma((2, 8)),
            dma((2, 8)),
            dma((n1,)),
            dma((n1,)),
            dma((n2,)),
            dma((n2,)),
            dma((n1,)),
            dma((n1,)),
        ],
        compiler_params=pltpu.CompilerParams(
            collective_id=0, has_side_effects=True, vmem_limit_bytes=48 * 1024 * 1024
        ),
        name="conv_silu_grads",
    )(inputs, weight, bias.reshape(1, ch), cotangent)
    return outputs, input_grad, weight_grad.reshape(3, 3, ch, ch), bias_grad.reshape(ch)


def solution(mesh):
    lons, lats = mesh.shape["lon"], mesh.shape["lat"]
    in_specs = (P("lat", "lon", None), P(), P(), P("lat", "lon", None))
    out_specs = (P("lat", "lon", None), P("lat", "lon", None), P(), P())
    return jax.shard_map(
        functools.partial(shards, lons, lats), mesh=mesh, in_specs=in_specs, out_specs=out_specs, check_vma=False
    )
```

```python
import functools
import math

import jax
import jax.numpy as jnp
from jax import lax
from jax.experimental import pallas as pl
from jax.experimental.pallas import tpu as pltpu
from jax.sharding import PartitionSpec as P

MESH = pl.DeviceIdType.MESH
F32 = jnp.float32
BF16 = jnp.bfloat16
CHUNK = 8
EXTRA = 16


def kernel(
    lons, lats, x_hbm, w_hbm, b_hbm, c_hbm,
    out_ref, gin_ref, wg_ref, bg_ref,
    x_ref, w_ref, b_ref, c_ref,
    xc, pc, pg, pgt, hrows, hcols, hcorn, hc32, scol32, scol, bacc,
    sbuf, r1, s2, r2, gath,
    lsem, ssem, rsem, s1sem, r1sem, s2sem, r2sem, s3sem, r3sem,
):
    pairs = ((x_hbm, x_ref), (w_hbm, w_ref), (b_hbm, b_ref), (c_hbm, c_ref))
    loads = [pltpu.make_async_copy(src, dst, lsem.at[i]) for i, (src, dst) in enumerate(pairs)]
    for load in loads:
        load.start()
    rows, cols, ch = x_ref.shape
    lon, lat = lax.axis_index("lon"), lax.axis_index("lat")
    half = lons // 2
    gl, gt = math.gcd(lons, 4), math.gcd(lats, 2)
    n1 = gl * gt
    n2 = (lons // gl) * (lats // gt)
    part = 3 * ch // n1

    top, bottom = lat == 0, lat == lats - 1
    n_lat = jnp.where(top, lat, lat - 1)
    s_lat = jnp.where(bottom, lat, lat + 1)
    n_lon = jnp.where(top, lon + half, lon)
    s_lon = jnp.where(bottom, lon + half, lon)

    def at(lon_at, lat_at):
        return (lax.rem(lon_at + lons, lons), lat_at)

    north, south = at(n_lon, n_lat), at(s_lon, s_lat)
    west, east = at(lon - 1, lat), at(lon + 1, lat)
    nw, ne = at(n_lon - 1, n_lat), at(n_lon + 1, n_lat)
    sw, se = at(s_lon - 1, s_lat), at(s_lon + 1, s_lat)

    g1 = lax.rem(lon, gl) * gt + lax.rem(lat, gt)
    g2 = (lon // gl) * (lats // gt) + lat // gt

    def peer1(k):
        q = lax.rem(g1 + k, n1)
        return q, ((lon // gl) * gl + q // gt, (lat // gt) * gt + lax.rem(q, gt))

    def peer2(k):
        q = lax.rem(g2 + k, n2)
        wide = lats // gt
        return q, ((q // wide) * gl + lax.rem(lon, gl), lax.rem(q, wide) * gt + lax.rem(lat, gt))

    barrier = pltpu.get_barrier_semaphore()
    greeted = [north, south, west, east, nw, ne, sw, se]
    greeted += [peer1(k)[1] for k in range(1, n1)] + [peer2(k)[1] for k in range(1, n2)]
    for device in greeted:
        pl.semaphore_signal(barrier, inc=1, device_id=device, device_id_type=MESH)

    def stage_columns(turn, src):
        def body(i, carry):
            for k in range(4):
                r = i * 4 + k
                scol32[0, pl.ds(r, 1), :] = src[r, 0:16, :].astype(F32)[0:1]
                scol32[1, pl.ds(r, 1), :] = src[r, cols - 16 : cols, :].astype(F32)[15:16]
            return carry

        lax.fori_loop(0, rows // 4, body, 0)
        scol[turn] = scol32[...].astype(BF16)

    def halo_copies(turn, src):
        lo, hi = slice(0, 16), slice(cols - 16, cols)
        to_north = jnp.where(top, 0, 1)
        to_south = jnp.where(bottom, 1, 0)
        to_nw, to_ne = jnp.where(top, 1, 3), jnp.where(top, 0, 2)
        to_sw, to_se = jnp.where(bottom, 3, 1), jnp.where(bottom, 2, 0)
        plan = [
            (scol.at[turn, 1], hcols.at[turn, 0], 2, east),
            (scol.at[turn, 0], hcols.at[turn, 1], 3, west),
            (src.at[0], hrows.at[turn, to_north], to_north, north),
            (src.at[rows - 1], hrows.at[turn, to_south], to_south, south),
            (src.at[0, lo, :], hcorn.at[turn, to_nw], 4 + to_nw, nw),
            (src.at[0, hi, :], hcorn.at[turn, to_ne], 4 + to_ne, ne),
            (src.at[rows - 1, lo, :], hcorn.at[turn, to_sw], 4 + to_sw, sw),
            (src.at[rows - 1, hi, :], hcorn.at[turn, to_se], 4 + to_se, se),
        ]
        return [
            pltpu.make_async_remote_copy(
                src_ref=s, dst_ref=d, send_sem=ssem.at[turn, i], recv_sem=rsem.at[turn, sem],
                device_id=device, device_id_type=MESH,
            )
            for i, (s, d, sem, device) in enumerate(plan)
        ]

    def halo_wait(turn):
        slots = [hrows.at[turn, 0], hrows.at[turn, 1], hcols.at[turn, 0], hcols.at[turn, 1]]
        slots += [hcorn.at[turn, i] for i in range(4)]
        for i, slot in enumerate(slots):
            pltpu.make_async_remote_copy(
                src_ref=slot, dst_ref=slot, send_sem=ssem.at[turn, i], recv_sem=rsem.at[turn, i],
                device_id=east, device_id_type=MESH,
            ).wait_recv()

    place = lax.broadcasted_iota(jnp.int32, (cols, ch), 0)

    def put_row(dst, at_row, centre, west_cell, east_cell):
        wide = centre.astype(F32)
        before = jnp.where(place == 0, west_cell, pltpu.roll(wide, 1, 0))
        after = jnp.where(place == cols - 1, east_cell, pltpu.roll(wide, cols - 1, 0))
        dst[at_row, :, 0:ch] = before.astype(BF16)
        dst[at_row, :, ch : 2 * ch] = centre
        dst[at_row, :, 2 * ch : 3 * ch] = after.astype(BF16)

    def widen(turn, src, dst):
        hc32[...] = hcols[turn].astype(F32)

        def body(i, carry):
            for k in range(4):
                r = i * 4 + k
                put_row(dst, r + 1, src[r], hc32[0, pl.ds(r, 1), :], hc32[1, pl.ds(r, 1), :])
            return carry

        lax.fori_loop(0, rows // 4, body, 0)
        for side, at_row in ((0, 0), (1, rows + 1)):
            west_cell = hcorn[turn, 2 * side].astype(F32)[15:16]
            east_cell = hcorn[turn, 2 * side + 1].astype(F32)[0:1]
            put_row(dst, at_row, hrows[turn, side], west_cell, east_cell)

    def windows(src, r0):
        return jnp.concatenate(
            [src[pl.ds(r0 + a, CHUNK)].reshape(CHUNK * cols, 3 * ch) for a in range(3)], axis=1
        )

    loads[0].wait()
    stage_columns(0, x_ref)
    pl.semaphore_wait(barrier, len(greeted))
    first = halo_copies(0, x_ref)
    for copy in first:
        copy.start()
    bacc[...] = jnp.zeros_like(bacc)
    for load in loads[1:]:
        load.wait()
    halo_wait(0)
    widen(0, x_ref, xc)

    def forward(i, carry):
        r0 = i * CHUNK
        lhs = windows(xc, r0)
        weight = w_ref[...].reshape(9 * ch, ch)
        pre = jnp.dot(lhs, weight, preferred_element_type=F32) + b_ref[...]
        sig = 1.0 / (1.0 + jnp.exp(-pre))
        out_ref[pl.ds(r0, CHUNK)] = (pre * sig).astype(BF16).reshape(CHUNK, cols, ch)
        cot = c_ref[pl.ds(r0, CHUNK)].reshape(CHUNK * cols, ch).astype(F32)
        grad = (cot * sig * (1.0 + pre * (1.0 - sig))).astype(BF16)
        pg[pl.ds(r0, CHUNK)] = grad.reshape(CHUNK, cols, ch)
        bacc[...] += jnp.sum(grad.astype(F32), axis=0, keepdims=True)
        pgt[:, pl.ds(pl.multiple_of(r0 * cols, ch), CHUNK * cols)] = grad.T
        return carry

    lax.fori_loop(0, rows // CHUNK, forward, 0)

    stage_columns(1, pg)
    second = halo_copies(1, pg)
    for copy in second:
        copy.start()

    line = lax.broadcasted_iota(jnp.int32, (EXTRA, ch), 0)

    def split(total):
        first_part = total.astype(BF16).astype(F32)
        rest = total - first_part
        second_part = rest.astype(BF16).astype(F32)
        third = rest - second_part
        rows_of = jnp.where(line == 0, first_part, jnp.where(line == 1, second_part, jnp.where(line == 2, third, 0.0)))
        return rows_of.astype(BF16)

    def lines(a):
        return part + EXTRA if a == 0 else part

    def wait_from(buffer, a, sems, send_sems, k, q):
        slot = buffer.at[a, q, 0 : lines(a)]
        pltpu.make_async_remote_copy(
            src_ref=slot, dst_ref=slot, send_sem=send_sems.at[a, k], recv_sem=sems.at[a, q],
            device_id=east, device_id_type=MESH,
        ).wait_recv()

    sent = []

    def send(src, dst, send_sem, recv_sem, device):
        copy = pltpu.make_async_remote_copy(
            src_ref=src, dst_ref=dst, send_sem=send_sem, recv_sem=recv_sem, device_id=device, device_id_type=MESH,
        )
        copy.start()
        sent.append(copy)

    def third(a):
        window = xc[a : a + rows].reshape(rows * cols, 3 * ch)
        grad = jnp.dot(pgt[...], window, preferred_element_type=F32)
        for b in range(3):
            block = grad[:, b * ch : (b + 1) * ch].T.astype(BF16)
            low = b * ch
            while low < (b + 1) * ch:
                q = low // part
                high = min((b + 1) * ch, (q + 1) * part)
                sbuf[a, q, low - q * part : high - q * part, :] = block[low - b * ch : high - b * ch]
                low = high
        if a == 0:
            bias_rows = split(bacc[...])
            for q in range(n1):
                sbuf[0, q, part : part + EXTRA, :] = bias_rows
        size = slice(0, lines(a))
        for k in range(1, n1):
            q, device = peer1(k)
            send(sbuf.at[a, q, size], r1.at[a, g1, size], s1sem.at[a, k], r1sem.at[a, g1], device)
        r1[a, g1, size, :] = sbuf[a, g1, size, :]

    def added(buffer, a, count):
        total = buffer[a, 0, 0 : lines(a), :].astype(F32)
        for q in range(1, count):
            total = total + buffer[a, q, 0 : lines(a), :].astype(F32)
        return total

    def along(a):
        for k in range(1, n1):
            wait_from(r1, a, r1sem, s1sem, k, peer1(k)[0])
        total = added(r1, a, n1)
        s2[a, 0:part, :] = total[:part].astype(BF16)
        if a == 0:
            s2[a, part : part + EXTRA, :] = split(jnp.sum(total[part:], axis=0, keepdims=True))
        size = slice(0, lines(a))
        for k in range(1, n2):
            q, device = peer2(k)
            send(s2.at[a, size], r2.at[a, g2, size], s2sem.at[a, k], r2sem.at[a, g2], device)
        r2[a, g2, size, :] = s2[a, size, :]

    scale = 1.0 / math.sqrt(rows * cols * lons * lats)

    def around(a):
        for k in range(1, n2):
            wait_from(r2, a, r2sem, s2sem, k, peer2(k)[0])
        total = added(r2, a, n2)
        if a == 0:
            bg_ref[...] = jnp.sum(total[part:], axis=0, keepdims=True) * scale
        gath[a, g1] = (total[:part] * scale).astype(BF16)
        for k in range(1, n1):
            q, device = peer1(k)
            send(gath.at[a, g1], gath.at[a, g1], s3sem.at[a, k], r3sem.at[a, g1], device)

    for a in range(3):
        third(a)

    halo_wait(1)
    widen(1, pg, pc)

    def kernel_for(taps):
        return jnp.concatenate([w_ref[a, b] for a in taps for b in (2, 1, 0)], axis=1)

    def back(lhs, rhs):
        return lax.dot_general(lhs, rhs, (((1,), (1,)), ((), ())), preferred_element_type=F32)

    def backward(i, carry):
        r0 = i * CHUNK
        grad = back(windows(pc, r0), kernel_for((2, 1, 0)))
        gin_ref[pl.ds(r0, CHUNK)] = grad.astype(BF16).reshape(CHUNK, cols, ch)
        return carry

    steps = rows // CHUNK
    lax.fori_loop(0, steps // 3, backward, 0)
    along(0)
    lax.fori_loop(steps // 3, 2 * steps // 3, backward, 0)
    along(1)
    around(0)
    lax.fori_loop(2 * steps // 3, steps, backward, 0)
    along(2)
    around(1)

    plain = kernel_for((2, 1, 0))
    lhs = jnp.concatenate([pc[a] for a in range(3)], axis=1)
    gin_ref[0] = back(lhs, jnp.where(top, kernel_for((0, 1, 0)), plain)).astype(BF16)
    lhs = jnp.concatenate([pc[rows - 1 + a] for a in range(3)], axis=1)
    gin_ref[rows - 1] = back(lhs, jnp.where(bottom, kernel_for((2, 1, 2)), plain)).astype(BF16)

    around(2)
    for a in range(3):
        for k in range(1, n1):
            q = peer1(k)[0]
            pltpu.make_async_remote_copy(
                src_ref=gath.at[a, q], dst_ref=gath.at[a, q], send_sem=s3sem.at[a, k], recv_sem=r3sem.at[a, q],
                device_id=east, device_id_type=MESH,
            ).wait_recv()
    wg_ref[...] = gath[...]
    for copy in first + second + sent:
        copy.wait_send()


def store(out_v, gin_v, wg_v, bg_v, out_hbm, gin_hbm, wg_hbm, bg_hbm, wide, sems):
    copies = [
        pltpu.make_async_copy(out_v, out_hbm, sems.at[0]),
        pltpu.make_async_copy(gin_v, gin_hbm, sems.at[1]),
        pltpu.make_async_copy(bg_v, bg_hbm, sems.at[2]),
        pltpu.make_async_copy(wide, wg_hbm, sems.at[3]),
    ]
    for copy in copies[:3]:
        copy.start()
    wide[...] = wg_v[...].astype(F32)
    copies[3].start()
    for copy in copies:
        copy.wait()


def shards(lons, lats, inputs, weight, bias, cotangent):
    rows, cols, ch = inputs.shape
    gl, gt = math.gcd(lons, 4), math.gcd(lats, 2)
    n1 = gl * gt
    n2 = (lons // gl) * (lats // gt)
    part = 3 * ch // n1
    vmem = pl.BlockSpec(memory_space=pltpu.VMEM)
    dma = pltpu.SemaphoreType.DMA
    anywhere = pl.BlockSpec(memory_space=pltpu.HBM)
    results = pl.pallas_call(
        functools.partial(kernel, lons, lats),
        out_shape=(
            jax.ShapeDtypeStruct((rows, cols, ch), BF16),
            jax.ShapeDtypeStruct((rows, cols, ch), BF16),
            jax.ShapeDtypeStruct((3, n1, part, ch), BF16),
            jax.ShapeDtypeStruct((1, ch), F32),
        ),
        in_specs=[anywhere] * 4,
        out_specs=(vmem,) * 4,
        scratch_shapes=[
            pltpu.VMEM((rows, cols, ch), BF16),
            pltpu.VMEM((3, 3, ch, ch), BF16),
            pltpu.VMEM((1, ch), F32),
            pltpu.VMEM((rows, cols, ch), BF16),
            pltpu.VMEM((rows + 2, cols, 3 * ch), BF16),
            pltpu.VMEM((rows + 2, cols, 3 * ch), BF16),
            pltpu.VMEM((rows, cols, ch), BF16),
            pltpu.VMEM((ch, rows * cols), BF16),
            pltpu.VMEM((2, 2, cols, ch), BF16),
            pltpu.VMEM((2, 2, rows, ch), BF16),
            pltpu.VMEM((2, 4, 16, ch), BF16),
            pltpu.VMEM((2, rows, ch), F32),
            pltpu.VMEM((2, rows, ch), F32),
            pltpu.VMEM((2, 2, rows, ch), BF16),
            pltpu.VMEM((1, ch), F32),
            pltpu.VMEM((3, n1, part + EXTRA, ch), BF16),
            pltpu.VMEM((3, n1, part + EXTRA, ch), BF16),
            pltpu.VMEM((3, part + EXTRA, ch), BF16),
            pltpu.VMEM((3, n2, part + EXTRA, ch), BF16),
            pltpu.VMEM((3, n1, part, ch), BF16),
            dma((4,)),
            dma((2, 8)),
            dma((2, 8)),
            dma((3, n1)),
            dma((3, n1)),
            dma((3, n2)),
            dma((3, n2)),
            dma((3, n1)),
            dma((3, n1)),
        ],
        compiler_params=pltpu.CompilerParams(
            collective_id=0, has_side_effects=True, vmem_limit_bytes=53 * 1024 * 1024
        ),
        name="conv_silu_grads",
    )(inputs, weight, bias.reshape(1, ch), cotangent)
    outputs, input_grad, weight_grad, bias_grad = pl.pallas_call(
        store,
        out_shape=(
            jax.ShapeDtypeStruct((rows, cols, ch), BF16),
            jax.ShapeDtypeStruct((rows, cols, ch), BF16),
            jax.ShapeDtypeStruct((3, n1, part, ch), F32),
            jax.ShapeDtypeStruct((1, ch), F32),
        ),
        in_specs=[vmem] * 4,
        out_specs=(anywhere,) * 4,
        scratch_shapes=[pltpu.VMEM((3, n1, part, ch), F32), dma((4,))],
        compiler_params=pltpu.CompilerParams(vmem_limit_bytes=48 * 1024 * 1024),
        name="write_results",
    )(*results)
    return outputs, input_grad, weight_grad.reshape(3, 3, ch, ch), bias_grad.reshape(ch)


def solution(mesh):
    lons, lats = mesh.shape["lon"], mesh.shape["lat"]
    in_specs = (P("lat", "lon", None), P(), P(), P("lat", "lon", None))
    out_specs = (P("lat", "lon", None), P("lat", "lon", None), P(), P())
    return jax.shard_map(
        functools.partial(shards, lons, lats), mesh=mesh, in_specs=in_specs, out_specs=out_specs, check_vma=False
    )
```

```python
import functools
import math

import jax
import jax.numpy as jnp
from jax import lax
from jax.experimental import pallas as pl
from jax.experimental.pallas import tpu as pltpu
from jax.sharding import PartitionSpec as P

MESH = pl.DeviceIdType.MESH
F32 = jnp.float32
BF16 = jnp.bfloat16
CHUNK = 16
EXTRA = 16


def kernel(
    lons, lats, x_hbm, w_hbm, b_hbm, c_hbm,
    out_hbm, gin_hbm, wg_hbm, bg_hbm,
    x_ref, w_ref, b_ref, c_ref, out_ref, gin_ref, wg_ref, bg_ref,
    vt, xc, pc, pg, pgt, hrows, hcols, hcorn, hc32, scol32, scol, bacc,
    sbuf, r1, s2, r2, gath,
    lsem, osem, ssem, rsem, s1sem, r1sem, s2sem, r2sem, s3sem, r3sem,
):
    pairs = ((x_hbm, x_ref), (w_hbm, w_ref), (b_hbm, b_ref), (c_hbm, c_ref))
    loads = [pltpu.make_async_copy(src, dst, lsem.at[i]) for i, (src, dst) in enumerate(pairs)]
    for load in loads:
        load.start()
    rows, cols, ch = x_ref.shape
    lon, lat = lax.axis_index("lon"), lax.axis_index("lat")
    half = lons // 2
    gl, gt = math.gcd(lons, 4), math.gcd(lats, 2)
    n1 = gl * gt
    n2 = (lons // gl) * (lats // gt)
    part = 3 * ch // n1

    top, bottom = lat == 0, lat == lats - 1
    n_lat = jnp.where(top, lat, lat - 1)
    s_lat = jnp.where(bottom, lat, lat + 1)
    n_lon = jnp.where(top, lon + half, lon)
    s_lon = jnp.where(bottom, lon + half, lon)

    def at(lon_at, lat_at):
        return (lax.rem(lon_at + lons, lons), lat_at)

    north, south = at(n_lon, n_lat), at(s_lon, s_lat)
    west, east = at(lon - 1, lat), at(lon + 1, lat)
    nw, ne = at(n_lon - 1, n_lat), at(n_lon + 1, n_lat)
    sw, se = at(s_lon - 1, s_lat), at(s_lon + 1, s_lat)

    g1 = lax.rem(lon, gl) * gt + lax.rem(lat, gt)
    g2 = (lon // gl) * (lats // gt) + lat // gt

    def peer1(k):
        q = lax.rem(g1 + k, n1)
        return q, ((lon // gl) * gl + q // gt, (lat // gt) * gt + lax.rem(q, gt))

    def peer2(k):
        q = lax.rem(g2 + k, n2)
        wide = lats // gt
        return q, ((q // wide) * gl + lax.rem(lon, gl), lax.rem(q, wide) * gt + lax.rem(lat, gt))

    barrier = pltpu.get_barrier_semaphore()
    greeted = [north, south, west, east, nw, ne, sw, se]
    greeted += [peer1(k)[1] for k in range(1, n1)] + [peer2(k)[1] for k in range(1, n2)]
    for device in greeted:
        pl.semaphore_signal(barrier, inc=1, device_id=device, device_id_type=MESH)

    def stage_columns(turn, src):
        def body(i, carry):
            for k in range(4):
                r = i * 4 + k
                scol32[0, pl.ds(r, 1), :] = src[r, 0:16, :].astype(F32)[0:1]
                scol32[1, pl.ds(r, 1), :] = src[r, cols - 16 : cols, :].astype(F32)[15:16]
            return carry

        lax.fori_loop(0, rows // 4, body, 0)
        scol[turn] = scol32[...].astype(BF16)

    def halo_copies(turn, src):
        lo, hi = slice(0, 16), slice(cols - 16, cols)
        to_north = jnp.where(top, 0, 1)
        to_south = jnp.where(bottom, 1, 0)
        to_nw, to_ne = jnp.where(top, 1, 3), jnp.where(top, 0, 2)
        to_sw, to_se = jnp.where(bottom, 3, 1), jnp.where(bottom, 2, 0)
        plan = [
            (scol.at[turn, 1], hcols.at[turn, 0], 2, east),
            (scol.at[turn, 0], hcols.at[turn, 1], 3, west),
            (src.at[0], hrows.at[turn, to_north], to_north, north),
            (src.at[rows - 1], hrows.at[turn, to_south], to_south, south),
            (src.at[0, lo, :], hcorn.at[turn, to_nw], 4 + to_nw, nw),
            (src.at[0, hi, :], hcorn.at[turn, to_ne], 4 + to_ne, ne),
            (src.at[rows - 1, lo, :], hcorn.at[turn, to_sw], 4 + to_sw, sw),
            (src.at[rows - 1, hi, :], hcorn.at[turn, to_se], 4 + to_se, se),
        ]
        return [
            pltpu.make_async_remote_copy(
                src_ref=s, dst_ref=d, send_sem=ssem.at[turn, i], recv_sem=rsem.at[turn, sem],
                device_id=device, device_id_type=MESH,
            )
            for i, (s, d, sem, device) in enumerate(plan)
        ]

    def halo_wait(turn):
        slots = [hrows.at[turn, 0], hrows.at[turn, 1], hcols.at[turn, 0], hcols.at[turn, 1]]
        slots += [hcorn.at[turn, i] for i in range(4)]
        for i, slot in enumerate(slots):
            pltpu.make_async_remote_copy(
                src_ref=slot, dst_ref=slot, send_sem=ssem.at[turn, i], recv_sem=rsem.at[turn, i],
                device_id=east, device_id_type=MESH,
            ).wait_recv()

    place = lax.broadcasted_iota(jnp.int32, (cols, ch), 0)

    def put_row(dst, at_row, centre, west_cell, east_cell):
        wide = centre.astype(F32)
        before = jnp.where(place == 0, west_cell, pltpu.roll(wide, 1, 0))
        after = jnp.where(place == cols - 1, east_cell, pltpu.roll(wide, cols - 1, 0))
        dst[at_row, :, 0:ch] = before.astype(BF16)
        dst[at_row, :, ch : 2 * ch] = centre
        dst[at_row, :, 2 * ch : 3 * ch] = after.astype(BF16)

    def widen(turn, src, dst):
        hc32[...] = hcols[turn].astype(F32)

        def body(i, carry):
            for k in range(4):
                r = i * 4 + k
                put_row(dst, r + 1, src[r], hc32[0, pl.ds(r, 1), :], hc32[1, pl.ds(r, 1), :])
            return carry

        lax.fori_loop(0, rows // 4, body, 0)
        for side, at_row in ((0, 0), (1, rows + 1)):
            west_cell = hcorn[turn, 2 * side].astype(F32)[15:16]
            east_cell = hcorn[turn, 2 * side + 1].astype(F32)[0:1]
            put_row(dst, at_row, hrows[turn, side], west_cell, east_cell)

    def windows(src, r0):
        return jnp.concatenate(
            [src[pl.ds(r0 + a, CHUNK)].reshape(CHUNK * cols, 3 * ch) for a in range(3)], axis=1
        )

    loads[0].wait()
    stage_columns(0, x_ref)
    pl.semaphore_wait(barrier, len(greeted))
    first = halo_copies(0, x_ref)
    for copy in first:
        copy.start()
    bacc[...] = jnp.zeros_like(bacc)
    for load in loads[1:]:
        load.wait()
    for a in range(3):
        for b in range(3):
            vt[(3 * a + b) * ch : (3 * a + b + 1) * ch, :] = w_ref[2 - a, 2 - b].T
    stores = []

    def store(src, dst):
        copy = pltpu.make_async_copy(src, dst, osem.at[len(stores)])
        copy.start()
        stores.append(copy)

    halo_wait(0)
    widen(0, x_ref, xc)

    def forward(i, carry):
        r0 = i * CHUNK
        lhs = windows(xc, r0)
        weight = w_ref[...].reshape(9 * ch, ch)
        pre = jnp.dot(lhs, weight, preferred_element_type=F32) + b_ref[...]
        sig = 0.5 * jnp.tanh(0.5 * pre) + 0.5
        out_ref[pl.ds(r0, CHUNK)] = (pre * sig).astype(BF16).reshape(CHUNK, cols, ch)
        cot = c_ref[pl.ds(r0, CHUNK)].reshape(CHUNK * cols, ch).astype(F32)
        grad = (cot * sig * (1.0 + pre * (1.0 - sig))).astype(BF16)
        pg[pl.ds(r0, CHUNK)] = grad.reshape(CHUNK, cols, ch)
        bacc[...] += jnp.sum(grad.astype(F32), axis=0, keepdims=True)
        pgt[:, pl.ds(pl.multiple_of(r0 * cols, ch), CHUNK * cols)] = grad.T
        return carry

    lax.fori_loop(0, rows // CHUNK, forward, 0)

    store(out_ref, out_hbm)
    stage_columns(1, pg)
    second = halo_copies(1, pg)
    for copy in second:
        copy.start()

    line = lax.broadcasted_iota(jnp.int32, (EXTRA, ch), 0)

    def split(total):
        first_part = total.astype(BF16).astype(F32)
        rest = total - first_part
        second_part = rest.astype(BF16).astype(F32)
        third = rest - second_part
        rows_of = jnp.where(line == 0, first_part, jnp.where(line == 1, second_part, jnp.where(line == 2, third, 0.0)))
        return rows_of.astype(BF16)

    def lines(a):
        return part + EXTRA if a == 0 else part

    def wait_from(buffer, a, sems, send_sems, k, q):
        slot = buffer.at[a, q, 0 : lines(a)]
        pltpu.make_async_remote_copy(
            src_ref=slot, dst_ref=slot, send_sem=send_sems.at[a, k], recv_sem=sems.at[a, q],
            device_id=east, device_id_type=MESH,
        ).wait_recv()

    sent = []

    def send(src, dst, send_sem, recv_sem, device):
        copy = pltpu.make_async_remote_copy(
            src_ref=src, dst_ref=dst, send_sem=send_sem, recv_sem=recv_sem, device_id=device, device_id_type=MESH,
        )
        copy.start()
        sent.append(copy)

    def third(a):
        window = xc[a : a + rows].reshape(rows * cols, 3 * ch)
        grad = jnp.dot(pgt[...], window, preferred_element_type=F32)
        for b in range(3):
            block = grad[:, b * ch : (b + 1) * ch].T.astype(BF16)
            low = b * ch
            while low < (b + 1) * ch:
                q = low // part
                high = min((b + 1) * ch, (q + 1) * part)
                sbuf[a, q, low - q * part : high - q * part, :] = block[low - b * ch : high - b * ch]
                low = high
        if a == 0:
            bias_rows = split(bacc[...])
            for q in range(n1):
                sbuf[0, q, part : part + EXTRA, :] = bias_rows
        size = slice(0, lines(a))
        for k in range(1, n1):
            q, device = peer1(k)
            send(sbuf.at[a, q, size], r1.at[a, g1, size], s1sem.at[a, k], r1sem.at[a, g1], device)
        r1[a, g1, size, :] = sbuf[a, g1, size, :]

    def added(buffer, a, count):
        total = buffer[a, 0, 0 : lines(a), :].astype(F32)
        for q in range(1, count):
            total = total + buffer[a, q, 0 : lines(a), :].astype(F32)
        return total

    def along(a):
        for k in range(1, n1):
            wait_from(r1, a, r1sem, s1sem, k, peer1(k)[0])
        total = added(r1, a, n1)
        s2[a, 0:part, :] = total[:part].astype(BF16)
        if a == 0:
            s2[a, part : part + EXTRA, :] = split(jnp.sum(total[part:], axis=0, keepdims=True))
        size = slice(0, lines(a))
        for k in range(1, n2):
            q, device = peer2(k)
            send(s2.at[a, size], r2.at[a, g2, size], s2sem.at[a, k], r2sem.at[a, g2], device)
        r2[a, g2, size, :] = s2[a, size, :]

    scale = 1.0 / math.sqrt(rows * cols * lons * lats)

    def around(a):
        for k in range(1, n2):
            wait_from(r2, a, r2sem, s2sem, k, peer2(k)[0])
        total = added(r2, a, n2)
        if a == 0:
            bg_ref[...] = jnp.sum(total[part:], axis=0, keepdims=True) * scale
            store(bg_ref, bg_hbm)
        gath[a, g1] = (total[:part] * scale).astype(BF16)
        for k in range(1, n1):
            q, device = peer1(k)
            send(gath.at[a, g1], gath.at[a, g1], s3sem.at[a, k], r3sem.at[a, g1], device)

    for a in range(3):
        third(a)

    halo_wait(1)
    widen(1, pg, pc)

    def backward(i, carry):
        r0 = i * CHUNK
        grad = jnp.dot(windows(pc, r0), vt[...], preferred_element_type=F32)
        gin_ref[pl.ds(r0, CHUNK)] = grad.astype(BF16).reshape(CHUNK, cols, ch)
        return carry

    steps = rows // CHUNK
    lax.fori_loop(0, steps // 3, backward, 0)
    along(0)
    lax.fori_loop(steps // 3, 2 * steps // 3, backward, 0)
    along(1)
    around(0)
    lax.fori_loop(2 * steps // 3, steps, backward, 0)
    along(2)
    around(1)

    def row_of(at_row, rhs):
        lhs = jnp.concatenate([pc[at_row + a] for a in range(3)], axis=1)
        gin_ref[at_row] = jnp.dot(lhs, rhs, preferred_element_type=F32).astype(BF16)

    third_of = 3 * ch
    near, far = vt[0:third_of, :], vt[2 * third_of :, :]
    row_of(0, jnp.concatenate([jnp.where(top, far, near), vt[third_of:, :]], axis=0))
    row_of(rows - 1, jnp.concatenate([vt[: 2 * third_of, :], jnp.where(bottom, near, far)], axis=0))
    store(gin_ref, gin_hbm)

    around(2)
    for a in range(3):
        for k in range(1, n1):
            q = peer1(k)[0]
            pltpu.make_async_remote_copy(
                src_ref=gath.at[a, q], dst_ref=gath.at[a, q], send_sem=s3sem.at[a, k], recv_sem=r3sem.at[a, q],
                device_id=east, device_id_type=MESH,
            ).wait_recv()
        wg_ref[a] = gath[a].astype(F32)
        store(wg_ref.at[a], wg_hbm.at[a])
    for copy in first + second + sent:
        copy.wait_send()
    for copy in stores:
        copy.wait()


def store_all(*refs):
    sems = refs[-1]
    count = len(refs) // 2
    copies = [pltpu.make_async_copy(refs[i], refs[count + i], sems.at[i]) for i in range(count)]
    for copy in copies:
        copy.start()
    for copy in copies:
        copy.wait()


def shards(lons, lats, inputs, weight, bias, cotangent):
    rows, cols, ch = inputs.shape
    gl, gt = math.gcd(lons, 4), math.gcd(lats, 2)
    n1 = gl * gt
    n2 = (lons // gl) * (lats // gt)
    part = 3 * ch // n1
    limit = 62 * 1024 * 1024
    dma = pltpu.SemaphoreType.DMA
    anywhere = pl.BlockSpec(memory_space=pltpu.HBM)
    results = pl.pallas_call(
        functools.partial(kernel, lons, lats),
        out_shape=(
            jax.ShapeDtypeStruct((rows, cols, ch), BF16),
            jax.ShapeDtypeStruct((rows, cols, ch), BF16),
            jax.ShapeDtypeStruct((3, n1, part, ch), F32),
            jax.ShapeDtypeStruct((1, ch), F32),
        ),
        in_specs=[anywhere] * 4,
        out_specs=(anywhere,) * 4,
        scratch_shapes=[
            pltpu.VMEM((rows, cols, ch), BF16),
            pltpu.VMEM((3, 3, ch, ch), BF16),
            pltpu.VMEM((1, ch), F32),
            pltpu.VMEM((rows, cols, ch), BF16),
            pltpu.VMEM((rows, cols, ch), BF16),
            pltpu.VMEM((rows, cols, ch), BF16),
            pltpu.VMEM((3, n1, part, ch), F32),
            pltpu.VMEM((1, ch), F32),
            pltpu.VMEM((9 * ch, ch), BF16),
            pltpu.VMEM((rows + 2, cols, 3 * ch), BF16),
            pltpu.VMEM((rows + 2, cols, 3 * ch), BF16),
            pltpu.VMEM((rows, cols, ch), BF16),
            pltpu.VMEM((ch, rows * cols), BF16),
            pltpu.VMEM((2, 2, cols, ch), BF16),
            pltpu.VMEM((2, 2, rows, ch), BF16),
            pltpu.VMEM((2, 4, 16, ch), BF16),
            pltpu.VMEM((2, rows, ch), F32),
            pltpu.VMEM((2, rows, ch), F32),
            pltpu.VMEM((2, 2, rows, ch), BF16),
            pltpu.VMEM((1, ch), F32),
            pltpu.VMEM((3, n1, part + EXTRA, ch), BF16),
            pltpu.VMEM((3, n1, part + EXTRA, ch), BF16),
            pltpu.VMEM((3, part + EXTRA, ch), BF16),
            pltpu.VMEM((3, n2, part + EXTRA, ch), BF16),
            pltpu.VMEM((3, n1, part, ch), BF16),
            dma((4,)),
            dma((6,)),
            dma((2, 8)),
            dma((2, 8)),
            dma((3, n1)),
            dma((3, n1)),
            dma((3, n2)),
            dma((3, n2)),
            dma((3, n1)),
            dma((3, n1)),
        ],
        compiler_params=pltpu.CompilerParams(
            collective_id=0, has_side_effects=True, vmem_limit_bytes=limit
        ),
        name="conv_silu_grads",
    )(inputs, weight, bias.reshape(1, ch), cotangent)
    outputs, input_grad, weight_grad, bias_grad = pl.pallas_call(
        store_all,
        out_shape=(
            jax.ShapeDtypeStruct((rows, cols, ch), BF16),
            jax.ShapeDtypeStruct((rows, cols, ch), BF16),
            jax.ShapeDtypeStruct((3, n1, part, ch), F32),
            jax.ShapeDtypeStruct((1, ch), F32),
        ),
        in_specs=[anywhere] * 4,
        out_specs=(anywhere,) * 4,
        scratch_shapes=[dma((4,))],
        compiler_params=pltpu.CompilerParams(vmem_limit_bytes=limit),
        name="write_results",
    )(*results)
    return outputs, input_grad, weight_grad.reshape(3, 3, ch, ch), bias_grad.reshape(ch)


def solution(mesh):
    lons, lats = mesh.shape["lon"], mesh.shape["lat"]
    in_specs = (P("lat", "lon", None), P(), P(), P("lat", "lon", None))
    out_specs = (P("lat", "lon", None), P("lat", "lon", None), P(), P())
    return jax.shard_map(
        functools.partial(shards, lons, lats), mesh=mesh, in_specs=in_specs, out_specs=out_specs, check_vma=False
    )
```

```python
import functools
import math

import jax
import jax.numpy as jnp
from jax import lax
from jax.experimental import pallas as pl
from jax.experimental.pallas import tpu as pltpu
from jax.sharding import PartitionSpec as P

MESH = pl.DeviceIdType.MESH
F32 = jnp.float32
BF16 = jnp.bfloat16
CHUNK = 16
EXTRA = 16


def kernel(
    lons, lats, x_hbm, w_hbm, b_hbm, c_hbm,
    out_hbm, gin_hbm, wg_hbm, bg_hbm,
    x_ref, w_ref, b_ref, c_ref, out_ref, gin_ref, wg_ref, bg_ref,
    vt, xc, pc, pg, pgt, hrows, hcols, hcorn, hc32, scol32, scol, ecol, fix, bacc,
    sbuf, r1, s2, r2, gath,
    lsem, osem, ssem, rsem, s1sem, r1sem, s2sem, r2sem, s3sem, r3sem,
):
    pairs = ((x_hbm, x_ref), (w_hbm, w_ref), (b_hbm, b_ref), (c_hbm, c_ref))
    loads = [pltpu.make_async_copy(src, dst, lsem.at[i]) for i, (src, dst) in enumerate(pairs)]
    for load in loads:
        load.start()
    rows, cols, ch = x_ref.shape
    lon, lat = lax.axis_index("lon"), lax.axis_index("lat")
    half = lons // 2
    gl, gt = math.gcd(lons, 4), math.gcd(lats, 2)
    n1 = gl * gt
    n2 = (lons // gl) * (lats // gt)
    part = 3 * ch // n1

    top, bottom = lat == 0, lat == lats - 1
    n_lat = jnp.where(top, lat, lat - 1)
    s_lat = jnp.where(bottom, lat, lat + 1)
    n_lon = jnp.where(top, lon + half, lon)
    s_lon = jnp.where(bottom, lon + half, lon)

    def at(lon_at, lat_at):
        return (lax.rem(lon_at + lons, lons), lat_at)

    north, south = at(n_lon, n_lat), at(s_lon, s_lat)
    west, east = at(lon - 1, lat), at(lon + 1, lat)
    nw, ne = at(n_lon - 1, n_lat), at(n_lon + 1, n_lat)
    sw, se = at(s_lon - 1, s_lat), at(s_lon + 1, s_lat)

    g1 = lax.rem(lon, gl) * gt + lax.rem(lat, gt)
    g2 = (lon // gl) * (lats // gt) + lat // gt

    def peer1(k):
        q = lax.rem(g1 + k, n1)
        return q, ((lon // gl) * gl + q // gt, (lat // gt) * gt + lax.rem(q, gt))

    def peer2(k):
        q = lax.rem(g2 + k, n2)
        wide = lats // gt
        return q, ((q // wide) * gl + lax.rem(lon, gl), lax.rem(q, wide) * gt + lax.rem(lat, gt))

    barrier = pltpu.get_barrier_semaphore()
    greeted = [north, south, west, east, nw, ne, sw, se]
    greeted += [peer1(k)[1] for k in range(1, n1)] + [peer2(k)[1] for k in range(1, n2)]
    for device in greeted:
        pl.semaphore_signal(barrier, inc=1, device_id=device, device_id_type=MESH)

    def stage_columns(src):
        def body(i, carry):
            for k in range(4):
                r = i * 4 + k
                scol32[0, pl.ds(r, 1), :] = src[r, 0:16, :].astype(F32)[0:1]
                scol32[1, pl.ds(r, 1), :] = src[r, cols - 16 : cols, :].astype(F32)[15:16]
            return carry

        lax.fori_loop(0, rows // 4, body, 0)

    def halo_copies(turn, src):
        lo, hi = slice(0, 16), slice(cols - 16, cols)
        to_north = jnp.where(top, 0, 1)
        to_south = jnp.where(bottom, 1, 0)
        to_nw, to_ne = jnp.where(top, 1, 3), jnp.where(top, 0, 2)
        to_sw, to_se = jnp.where(bottom, 3, 1), jnp.where(bottom, 2, 0)
        plan = [
            (scol.at[turn, 1], hcols.at[turn, 0], 2, east),
            (scol.at[turn, 0], hcols.at[turn, 1], 3, west),
            (src.at[0], hrows.at[turn, to_north], to_north, north),
            (src.at[rows - 1], hrows.at[turn, to_south], to_south, south),
            (src.at[0, lo, :], hcorn.at[turn, to_nw], 4 + to_nw, nw),
            (src.at[0, hi, :], hcorn.at[turn, to_ne], 4 + to_ne, ne),
            (src.at[rows - 1, lo, :], hcorn.at[turn, to_sw], 4 + to_sw, sw),
            (src.at[rows - 1, hi, :], hcorn.at[turn, to_se], 4 + to_se, se),
        ]
        return [
            pltpu.make_async_remote_copy(
                src_ref=s, dst_ref=d, send_sem=ssem.at[turn, i], recv_sem=rsem.at[turn, sem],
                device_id=device, device_id_type=MESH,
            )
            for i, (s, d, sem, device) in enumerate(plan)
        ]

    def halo_wait(turn):
        slots = [hrows.at[turn, 0], hrows.at[turn, 1], hcols.at[turn, 0], hcols.at[turn, 1]]
        slots += [hcorn.at[turn, i] for i in range(4)]
        for i, slot in enumerate(slots):
            pltpu.make_async_remote_copy(
                src_ref=slot, dst_ref=slot, send_sem=ssem.at[turn, i], recv_sem=rsem.at[turn, i],
                device_id=east, device_id_type=MESH,
            ).wait_recv()

    place = lax.broadcasted_iota(jnp.int32, (cols, ch), 0)

    def put_row(dst, at_row, centre, west_cell, east_cell):
        wide = centre.astype(F32)
        before = jnp.where(place == 0, west_cell, pltpu.roll(wide, 1, 0))
        after = jnp.where(place == cols - 1, east_cell, pltpu.roll(wide, cols - 1, 0))
        dst[at_row, :, 0:ch] = before.astype(BF16)
        dst[at_row, :, ch : 2 * ch] = centre
        dst[at_row, :, 2 * ch : 3 * ch] = after.astype(BF16)

    def widen(turn, src, dst):
        hc32[...] = hcols[turn].astype(F32)

        def body(i, carry):
            for k in range(4):
                r = i * 4 + k
                put_row(dst, r + 1, src[r], hc32[0, pl.ds(r, 1), :], hc32[1, pl.ds(r, 1), :])
            return carry

        lax.fori_loop(0, rows // 4, body, 0)
        for side, at_row in ((0, 0), (1, rows + 1)):
            west_cell = hcorn[turn, 2 * side].astype(F32)[15:16]
            east_cell = hcorn[turn, 2 * side + 1].astype(F32)[0:1]
            put_row(dst, at_row, hrows[turn, side], west_cell, east_cell)

    def windows(src, r0):
        return jnp.concatenate(
            [src[pl.ds(r0 + a, CHUNK)].reshape(CHUNK * cols, 3 * ch) for a in range(3)], axis=1
        )

    loads[0].wait()
    stage_columns(x_ref)
    scol[0] = scol32[...].astype(BF16)
    pl.semaphore_wait(barrier, len(greeted))
    first = halo_copies(0, x_ref)
    for copy in first:
        copy.start()

    nothing = jnp.zeros((1, ch), F32)

    def widen_alone(i, carry):
        for k in range(4):
            put_row(xc, i * 4 + k + 1, x_ref[i * 4 + k], nothing, nothing)
        return carry

    lax.fori_loop(0, rows // 4, widen_alone, 0)
    xc[0] = jnp.zeros((cols, 3 * ch), BF16)
    xc[rows + 1] = jnp.zeros((cols, 3 * ch), BF16)
    bacc[...] = jnp.zeros_like(bacc)
    for load in loads[1:]:
        load.wait()
    stores = []

    def store(src, dst):
        copy = pltpu.make_async_copy(src, dst, osem.at[len(stores)])
        copy.start()
        stores.append(copy)

    def layer(lhs, cot):
        pre = jnp.dot(lhs, w_ref[...].reshape(9 * ch, ch), preferred_element_type=F32) + b_ref[...]
        sig = 0.5 * jnp.tanh(0.5 * pre) + 0.5
        return pre * sig, cot * sig * (1.0 + pre * (1.0 - sig))

    def forward(i, carry):
        r0 = i * CHUNK
        cot = c_ref[pl.ds(r0, CHUNK)].reshape(CHUNK * cols, ch).astype(F32)
        value, grad = layer(windows(xc, r0), cot)
        out_ref[pl.ds(r0, CHUNK)] = value.astype(BF16).reshape(CHUNK, cols, ch)
        pg[pl.ds(r0, CHUNK)] = grad.astype(BF16).reshape(CHUNK, cols, ch)
        return carry

    lax.fori_loop(0, rows // CHUNK, forward, 0)
    for a in range(3):
        for b in range(3):
            vt[(3 * a + b) * ch : (3 * a + b + 1) * ch, :] = w_ref[2 - a, 2 - b].T
    stage_columns(c_ref)

    halo_wait(0)
    hc32[...] = hcols[0].astype(F32)
    for side, at_row in ((0, 0), (1, rows + 1)):
        west_cell = hcorn[0, 2 * side].astype(F32)[15:16]
        east_cell = hcorn[0, 2 * side + 1].astype(F32)[0:1]
        put_row(xc, at_row, hrows[0, side], west_cell, east_cell)
        ecol[0, at_row : at_row + 1, :] = xc[at_row, 0:16, :].astype(F32)[0:1]
        ecol[1, at_row : at_row + 1, :] = xc[at_row, cols - 16 : cols, :].astype(F32)[15:16]
    tile = lax.broadcasted_iota(jnp.int32, (16, ch), 0)

    def patch(i, carry):
        for k in range(4):
            r = i * 4 + k
            left, right = hc32[0, pl.ds(r, 1), :], hc32[1, pl.ds(r, 1), :]
            edge = xc[r + 1, 0:16, :].astype(F32)
            ecol[0, pl.ds(r + 1, 1), :] = jnp.concatenate([left, edge[0:1, ch:]], axis=1)
            xc[r + 1, 0:16, 0:ch] = jnp.where(tile == 0, left, edge[:, 0:ch]).astype(BF16)
            edge = xc[r + 1, cols - 16 : cols, :].astype(F32)
            ecol[1, pl.ds(r + 1, 1), :] = jnp.concatenate([edge[15:16, : 2 * ch], right], axis=1)
            xc[r + 1, cols - 16 : cols, 2 * ch :] = jnp.where(tile == 15, right, edge[:, 2 * ch :]).astype(BF16)
        return carry

    lax.fori_loop(0, rows // 4, patch, 0)
    lhs = [jnp.concatenate([xc[r + a] for a in range(3)], axis=1) for r in (0, rows - 1)]
    for side in range(2):
        lhs.append(jnp.concatenate([ecol[side, a : a + rows, :] for a in range(3)], axis=1).astype(BF16))
    cot = [c_ref[0].astype(F32), c_ref[rows - 1].astype(F32), scol32[0], scol32[1]]
    value, grad = layer(jnp.concatenate(lhs, axis=0), jnp.concatenate(cot, axis=0))
    out_ref[0] = value[0:cols].astype(BF16)
    out_ref[rows - 1] = value[cols : 2 * cols].astype(BF16)
    pg[0] = grad[0:cols].astype(BF16)
    pg[rows - 1] = grad[cols : 2 * cols].astype(BF16)
    for side in range(2):
        low = 2 * cols + side * rows
        fix[0, side] = value[low : low + rows]
        fix[1, side] = grad[low : low + rows]
        scol[1, side] = grad[low : low + rows].astype(BF16)

    def put_columns(i, carry):
        for k in range(4):
            r = i * 4 + k
            for which, ref in ((0, out_ref), (1, pg)):
                for side, start, line_at in ((0, 0, 0), (1, cols - 16, 15)):
                    old = ref[r, start : start + 16, :].astype(F32)
                    new = jnp.where(tile == line_at, fix[which, side, pl.ds(r, 1), :], old)
                    ref[r, start : start + 16, :] = new.astype(BF16)
        return carry

    lax.fori_loop(0, rows // 4, put_columns, 0)

    second = halo_copies(1, pg)
    for copy in second:
        copy.start()
    store(out_ref, out_hbm)

    def turn_over(i, carry):
        r0 = i * CHUNK
        grad = pg[pl.ds(r0, CHUNK)].reshape(CHUNK * cols, ch)
        bacc[...] += jnp.sum(grad.astype(F32), axis=0, keepdims=True)
        pgt[:, pl.ds(pl.multiple_of(r0 * cols, ch), CHUNK * cols)] = grad.T
        return carry

    lax.fori_loop(0, rows // CHUNK, turn_over, 0)

    line = lax.broadcasted_iota(jnp.int32, (EXTRA, ch), 0)

    def split(total):
        first_part = total.astype(BF16).astype(F32)
        rest = total - first_part
        second_part = rest.astype(BF16).astype(F32)
        third = rest - second_part
        rows_of = jnp.where(line == 0, first_part, jnp.where(line == 1, second_part, jnp.where(line == 2, third, 0.0)))
        return rows_of.astype(BF16)

    def lines(a):
        return part + EXTRA if a == 0 else part

    def wait_from(buffer, a, sems, send_sems, k, q):
        slot = buffer.at[a, q, 0 : lines(a)]
        pltpu.make_async_remote_copy(
            src_ref=slot, dst_ref=slot, send_sem=send_sems.at[a, k], recv_sem=sems.at[a, q],
            device_id=east, device_id_type=MESH,
        ).wait_recv()

    sent = []

    def send(src, dst, send_sem, recv_sem, device):
        copy = pltpu.make_async_remote_copy(
            src_ref=src, dst_ref=dst, send_sem=send_sem, recv_sem=recv_sem, device_id=device, device_id_type=MESH,
        )
        copy.start()
        sent.append(copy)

    def third(a):
        window = xc[a : a + rows].reshape(rows * cols, 3 * ch)
        grad = jnp.dot(pgt[...], window, preferred_element_type=F32)
        for b in range(3):
            block = grad[:, b * ch : (b + 1) * ch].T.astype(BF16)
            low = b * ch
            while low < (b + 1) * ch:
                q = low // part
                high = min((b + 1) * ch, (q + 1) * part)
                sbuf[a, q, low - q * part : high - q * part, :] = block[low - b * ch : high - b * ch]
                low = high
        if a == 0:
            bias_rows = split(bacc[...])
            for q in range(n1):
                sbuf[0, q, part : part + EXTRA, :] = bias_rows
        size = slice(0, lines(a))
        for k in range(1, n1):
            q, device = peer1(k)
            send(sbuf.at[a, q, size], r1.at[a, g1, size], s1sem.at[a, k], r1sem.at[a, g1], device)
        r1[a, g1, size, :] = sbuf[a, g1, size, :]

    def added(buffer, a, count):
        total = buffer[a, 0, 0 : lines(a), :].astype(F32)
        for q in range(1, count):
            total = total + buffer[a, q, 0 : lines(a), :].astype(F32)
        return total

    def along(a):
        for k in range(1, n1):
            wait_from(r1, a, r1sem, s1sem, k, peer1(k)[0])
        total = added(r1, a, n1)
        s2[a, 0:part, :] = total[:part].astype(BF16)
        if a == 0:
            s2[a, part : part + EXTRA, :] = split(jnp.sum(total[part:], axis=0, keepdims=True))
        size = slice(0, lines(a))
        for k in range(1, n2):
            q, device = peer2(k)
            send(s2.at[a, size], r2.at[a, g2, size], s2sem.at[a, k], r2sem.at[a, g2], device)
        r2[a, g2, size, :] = s2[a, size, :]

    scale = 1.0 / math.sqrt(rows * cols * lons * lats)

    def around(a):
        for k in range(1, n2):
            wait_from(r2, a, r2sem, s2sem, k, peer2(k)[0])
        total = added(r2, a, n2)
        if a == 0:
            bg_ref[...] = jnp.sum(total[part:], axis=0, keepdims=True) * scale
            store(bg_ref, bg_hbm)
        gath[a, g1] = (total[:part] * scale).astype(BF16)
        for k in range(1, n1):
            q, device = peer1(k)
            send(gath.at[a, g1], gath.at[a, g1], s3sem.at[a, k], r3sem.at[a, g1], device)

    for a in range(3):
        third(a)

    halo_wait(1)
    widen(1, pg, pc)

    def backward(i, carry):
        r0 = i * CHUNK
        grad = jnp.dot(windows(pc, r0), vt[...], preferred_element_type=F32)
        gin_ref[pl.ds(r0, CHUNK)] = grad.astype(BF16).reshape(CHUNK, cols, ch)
        return carry

    steps = rows // CHUNK
    lax.fori_loop(0, steps // 3, backward, 0)
    along(0)
    lax.fori_loop(steps // 3, 2 * steps // 3, backward, 0)
    along(1)
    around(0)
    lax.fori_loop(2 * steps // 3, steps, backward, 0)
    along(2)
    around(1)

    def row_of(at_row, rhs):
        lhs = jnp.concatenate([pc[at_row + a] for a in range(3)], axis=1)
        gin_ref[at_row] = jnp.dot(lhs, rhs, preferred_element_type=F32).astype(BF16)

    third_of = 3 * ch
    near, far = vt[0:third_of, :], vt[2 * third_of :, :]
    row_of(0, jnp.concatenate([jnp.where(top, far, near), vt[third_of:, :]], axis=0))
    row_of(rows - 1, jnp.concatenate([vt[: 2 * third_of, :], jnp.where(bottom, near, far)], axis=0))
    store(gin_ref, gin_hbm)

    around(2)
    for a in range(3):
        for k in range(1, n1):
            q = peer1(k)[0]
            pltpu.make_async_remote_copy(
                src_ref=gath.at[a, q], dst_ref=gath.at[a, q], send_sem=s3sem.at[a, k], recv_sem=r3sem.at[a, q],
                device_id=east, device_id_type=MESH,
            ).wait_recv()
        wg_ref[a] = gath[a].astype(F32)
        store(wg_ref.at[a], wg_hbm.at[a])
    for copy in first + second + sent:
        copy.wait_send()
    for copy in stores:
        copy.wait()


def store_all(*refs):
    sources, targets, staged, sems = refs[0:4], refs[4:8], refs[8:12], refs[12]
    loads = [pltpu.make_async_copy(s, v, sems.at[0, i]) for i, (s, v) in enumerate(zip(sources, staged))]
    stores = [pltpu.make_async_copy(v, t, sems.at[1, i]) for i, (v, t) in enumerate(zip(staged, targets))]
    for load in loads:
        load.start()
    for load, save in zip(loads, stores):
        load.wait()
        save.start()
    for save in stores:
        save.wait()


def shards(lons, lats, inputs, weight, bias, cotangent):
    rows, cols, ch = inputs.shape
    gl, gt = math.gcd(lons, 4), math.gcd(lats, 2)
    n1 = gl * gt
    n2 = (lons // gl) * (lats // gt)
    part = 3 * ch // n1
    limit = 62 * 1024 * 1024
    dma = pltpu.SemaphoreType.DMA
    anywhere = pl.BlockSpec(memory_space=pltpu.HBM)
    results = pl.pallas_call(
        functools.partial(kernel, lons, lats),
        out_shape=(
            jax.ShapeDtypeStruct((rows, cols, ch), BF16),
            jax.ShapeDtypeStruct((rows, cols, ch), BF16),
            jax.ShapeDtypeStruct((3, n1, part, ch), F32),
            jax.ShapeDtypeStruct((1, ch), F32),
        ),
        in_specs=[anywhere] * 4,
        out_specs=(anywhere,) * 4,
        scratch_shapes=[
            pltpu.VMEM((rows, cols, ch), BF16),
            pltpu.VMEM((3, 3, ch, ch), BF16),
            pltpu.VMEM((1, ch), F32),
            pltpu.VMEM((rows, cols, ch), BF16),
            pltpu.VMEM((rows, cols, ch), BF16),
            pltpu.VMEM((rows, cols, ch), BF16),
            pltpu.VMEM((3, n1, part, ch), F32),
            pltpu.VMEM((1, ch), F32),
            pltpu.VMEM((9 * ch, ch), BF16),
            pltpu.VMEM((rows + 2, cols, 3 * ch), BF16),
            pltpu.VMEM((rows + 2, cols, 3 * ch), BF16),
            pltpu.VMEM((rows, cols, ch), BF16),
            pltpu.VMEM((ch, rows * cols), BF16),
            pltpu.VMEM((2, 2, cols, ch), BF16),
            pltpu.VMEM((2, 2, rows, ch), BF16),
            pltpu.VMEM((2, 4, 16, ch), BF16),
            pltpu.VMEM((2, rows, ch), F32),
            pltpu.VMEM((2, rows, ch), F32),
            pltpu.VMEM((2, 2, rows, ch), BF16),
            pltpu.VMEM((2, rows + 2, 3 * ch), F32),
            pltpu.VMEM((2, 2, rows, ch), F32),
            pltpu.VMEM((1, ch), F32),
            pltpu.VMEM((3, n1, part + EXTRA, ch), BF16),
            pltpu.VMEM((3, n1, part + EXTRA, ch), BF16),
            pltpu.VMEM((3, part + EXTRA, ch), BF16),
            pltpu.VMEM((3, n2, part + EXTRA, ch), BF16),
            pltpu.VMEM((3, n1, part, ch), BF16),
            dma((4,)),
            dma((6,)),
            dma((2, 8)),
            dma((2, 8)),
            dma((3, n1)),
            dma((3, n1)),
            dma((3, n2)),
            dma((3, n2)),
            dma((3, n1)),
            dma((3, n1)),
        ],
        compiler_params=pltpu.CompilerParams(
            collective_id=0, has_side_effects=True, vmem_limit_bytes=limit
        ),
        name="conv_silu_grads",
    )(inputs, weight, bias.reshape(1, ch), cotangent)
    outputs, input_grad, weight_grad, bias_grad = pl.pallas_call(
        store_all,
        out_shape=(
            jax.ShapeDtypeStruct((rows, cols, ch), BF16),
            jax.ShapeDtypeStruct((rows, cols, ch), BF16),
            jax.ShapeDtypeStruct((3, n1, part, ch), F32),
            jax.ShapeDtypeStruct((1, ch), F32),
        ),
        in_specs=[anywhere] * 4,
        out_specs=(anywhere,) * 4,
        scratch_shapes=[
            pltpu.VMEM((rows, cols, ch), BF16),
            pltpu.VMEM((rows, cols, ch), BF16),
            pltpu.VMEM((3, n1, part, ch), F32),
            pltpu.VMEM((1, ch), F32),
            dma((2, 4)),
        ],
        compiler_params=pltpu.CompilerParams(vmem_limit_bytes=limit),
        name="write_results",
    )(*results)
    return outputs, input_grad, weight_grad.reshape(3, 3, ch, ch), bias_grad.reshape(ch)


def solution(mesh):
    lons, lats = mesh.shape["lon"], mesh.shape["lat"]
    in_specs = (P("lat", "lon", None), P(), P(), P("lat", "lon", None))
    out_specs = (P("lat", "lon", None), P("lat", "lon", None), P(), P())
    return jax.shard_map(
        functools.partial(shards, lons, lats), mesh=mesh, in_specs=in_specs, out_specs=out_specs, check_vma=False
    )
```

```python
import functools
import math

import jax
import jax.numpy as jnp
from jax import lax
from jax.experimental import pallas as pl
from jax.experimental.pallas import tpu as pltpu
from jax.sharding import PartitionSpec as P

MESH = pl.DeviceIdType.MESH
F32 = jnp.float32
BF16 = jnp.bfloat16
CHUNK = 16
EXTRA = 16


def kernel(
    lons, lats, x_hbm, w_hbm, b_hbm, c_hbm,
    out_hbm, gin_hbm, wg_hbm, bg_hbm,
    x_ref, w_ref, b_ref, c_ref, out_ref, gin_ref, wg_ref, bg_ref,
    vt, xc, pc, pg, pgt, hrows, hcols, hcorn, hc32, scol32, scol, ecol, fix, bacc,
    sbuf, r0, s1, r1, s2, r2, gath,
    lsem, osem, ssem, rsem, gsem,
):
    pairs = ((x_hbm, x_ref), (w_hbm, w_ref), (b_hbm, b_ref), (c_hbm, c_ref))
    loads = [pltpu.make_async_copy(src, dst, lsem.at[i]) for i, (src, dst) in enumerate(pairs)]
    for load in loads:
        load.start()
    rows, cols, ch = x_ref.shape
    lon, lat = lax.axis_index("lon"), lax.axis_index("lat")
    half = lons // 2
    gl, gt = math.gcd(lons, 4), math.gcd(lats, 2)
    chips = (gl // 2) * gt
    n2 = (lons // gl) * (lats // gt)
    part = 3 * ch // (2 * chips)

    top, bottom = lat == 0, lat == lats - 1
    n_lat = jnp.where(top, lat, lat - 1)
    s_lat = jnp.where(bottom, lat, lat + 1)
    n_lon = jnp.where(top, lon + half, lon)
    s_lon = jnp.where(bottom, lon + half, lon)

    def at(lon_at, lat_at):
        return (lax.rem(lon_at + lons, lons), lat_at)

    north, south = at(n_lon, n_lat), at(s_lon, s_lat)
    west, east = at(lon - 1, lat), at(lon + 1, lat)
    nw, ne = at(n_lon - 1, n_lat), at(n_lon + 1, n_lat)
    sw, se = at(s_lon - 1, s_lat), at(s_lon + 1, s_lat)

    core = lax.rem(lon, 2)
    sibling = (lon + 1 - 2 * core, lat)
    g1 = (lax.rem(lon, gl) // 2) * gt + lax.rem(lat, gt)
    g2 = (lon // gl) * (lats // gt) + lat // gt

    def peer1(k):
        q = lax.rem(g1 + k, chips)
        return q, ((lon // gl) * gl + (q // gt) * 2 + core, (lat // gt) * gt + lax.rem(q, gt))

    def peer2(k):
        q = lax.rem(g2 + k, n2)
        wide = lats // gt
        return q, ((q // wide) * gl + lax.rem(lon, gl), lax.rem(q, wide) * gt + lax.rem(lat, gt))

    barrier = pltpu.get_barrier_semaphore()
    greeted = [north, south, west, east, nw, ne, sw, se]
    greeted += [sibling] + [peer1(k)[1] for k in range(1, chips)] + [peer2(k)[1] for k in range(1, n2)]
    for device in greeted:
        pl.semaphore_signal(barrier, inc=1, device_id=device, device_id_type=MESH)

    def stage_columns(src):
        def body(i, carry):
            for k in range(4):
                r = i * 4 + k
                scol32[0, pl.ds(r, 1), :] = src[r, 0:16, :].astype(F32)[0:1]
                scol32[1, pl.ds(r, 1), :] = src[r, cols - 16 : cols, :].astype(F32)[15:16]
            return carry

        lax.fori_loop(0, rows // 4, body, 0)

    def halo_copies(turn, src):
        lo, hi = slice(0, 16), slice(cols - 16, cols)
        to_north = jnp.where(top, 0, 1)
        to_south = jnp.where(bottom, 1, 0)
        to_nw, to_ne = jnp.where(top, 1, 3), jnp.where(top, 0, 2)
        to_sw, to_se = jnp.where(bottom, 3, 1), jnp.where(bottom, 2, 0)
        plan = [
            (scol.at[turn, 1], hcols.at[turn, 0], 2, east),
            (scol.at[turn, 0], hcols.at[turn, 1], 3, west),
            (src.at[0], hrows.at[turn, to_north], to_north, north),
            (src.at[rows - 1], hrows.at[turn, to_south], to_south, south),
            (src.at[0, lo, :], hcorn.at[turn, to_nw], 4 + to_nw, nw),
            (src.at[0, hi, :], hcorn.at[turn, to_ne], 4 + to_ne, ne),
            (src.at[rows - 1, lo, :], hcorn.at[turn, to_sw], 4 + to_sw, sw),
            (src.at[rows - 1, hi, :], hcorn.at[turn, to_se], 4 + to_se, se),
        ]
        return [
            pltpu.make_async_remote_copy(
                src_ref=s, dst_ref=d, send_sem=ssem.at[turn, i], recv_sem=rsem.at[turn, sem],
                device_id=device, device_id_type=MESH,
            )
            for i, (s, d, sem, device) in enumerate(plan)
        ]

    def halo_wait(turn):
        slots = [hrows.at[turn, 0], hrows.at[turn, 1], hcols.at[turn, 0], hcols.at[turn, 1]]
        slots += [hcorn.at[turn, i] for i in range(4)]
        for i, slot in enumerate(slots):
            pltpu.make_async_remote_copy(
                src_ref=slot, dst_ref=slot, send_sem=ssem.at[turn, i], recv_sem=rsem.at[turn, i],
                device_id=east, device_id_type=MESH,
            ).wait_recv()

    place = lax.broadcasted_iota(jnp.int32, (cols, ch), 0)

    def put_row(dst, at_row, centre, west_cell, east_cell):
        wide = centre.astype(F32)
        before = jnp.where(place == 0, west_cell, pltpu.roll(wide, 1, 0))
        after = jnp.where(place == cols - 1, east_cell, pltpu.roll(wide, cols - 1, 0))
        dst[at_row, :, 0:ch] = before.astype(BF16)
        dst[at_row, :, ch : 2 * ch] = centre
        dst[at_row, :, 2 * ch : 3 * ch] = after.astype(BF16)

    def widen(turn, src, dst):
        hc32[...] = hcols[turn].astype(F32)

        def body(i, carry):
            for k in range(4):
                r = i * 4 + k
                put_row(dst, r + 1, src[r], hc32[0, pl.ds(r, 1), :], hc32[1, pl.ds(r, 1), :])
            return carry

        lax.fori_loop(0, rows // 4, body, 0)
        for side, at_row in ((0, 0), (1, rows + 1)):
            west_cell = hcorn[turn, 2 * side].astype(F32)[15:16]
            east_cell = hcorn[turn, 2 * side + 1].astype(F32)[0:1]
            put_row(dst, at_row, hrows[turn, side], west_cell, east_cell)

    def windows(src, r0):
        return jnp.concatenate(
            [src[pl.ds(r0 + a, CHUNK)].reshape(CHUNK * cols, 3 * ch) for a in range(3)], axis=1
        )

    loads[0].wait()
    stage_columns(x_ref)
    scol[0] = scol32[...].astype(BF16)
    pl.semaphore_wait(barrier, len(greeted))
    first = halo_copies(0, x_ref)
    for copy in first:
        copy.start()

    nothing = jnp.zeros((1, ch), F32)

    def widen_alone(i, carry):
        for k in range(4):
            put_row(xc, i * 4 + k + 1, x_ref[i * 4 + k], nothing, nothing)
        return carry

    lax.fori_loop(0, rows // 4, widen_alone, 0)
    xc[0] = jnp.zeros((cols, 3 * ch), BF16)
    xc[rows + 1] = jnp.zeros((cols, 3 * ch), BF16)
    bacc[...] = jnp.zeros_like(bacc)
    for load in loads[1:]:
        load.wait()
    stores = []

    def store(src, dst):
        copy = pltpu.make_async_copy(src, dst, osem.at[len(stores)])
        copy.start()
        stores.append(copy)

    def layer(lhs, cot):
        pre = jnp.dot(lhs, w_ref[...].reshape(9 * ch, ch), preferred_element_type=F32) + b_ref[...]
        sig = 0.5 * jnp.tanh(0.5 * pre) + 0.5
        return pre * sig, cot * sig * (1.0 + pre * (1.0 - sig))

    def forward(i, carry):
        r0 = i * CHUNK
        cot = c_ref[pl.ds(r0, CHUNK)].reshape(CHUNK * cols, ch).astype(F32)
        value, grad = layer(windows(xc, r0), cot)
        out_ref[pl.ds(r0, CHUNK)] = value.astype(BF16).reshape(CHUNK, cols, ch)
        pg[pl.ds(r0, CHUNK)] = grad.astype(BF16).reshape(CHUNK, cols, ch)
        return carry

    lax.fori_loop(0, rows // CHUNK, forward, 0)
    for a in range(3):
        for b in range(3):
            vt[(3 * a + b) * ch : (3 * a + b + 1) * ch, :] = w_ref[2 - a, 2 - b].T
    stage_columns(c_ref)

    halo_wait(0)
    hc32[...] = hcols[0].astype(F32)
    for side, at_row in ((0, 0), (1, rows + 1)):
        west_cell = hcorn[0, 2 * side].astype(F32)[15:16]
        east_cell = hcorn[0, 2 * side + 1].astype(F32)[0:1]
        put_row(xc, at_row, hrows[0, side], west_cell, east_cell)
        ecol[0, at_row : at_row + 1, :] = xc[at_row, 0:16, :].astype(F32)[0:1]
        ecol[1, at_row : at_row + 1, :] = xc[at_row, cols - 16 : cols, :].astype(F32)[15:16]
    tile = lax.broadcasted_iota(jnp.int32, (16, ch), 0)

    def patch(i, carry):
        for k in range(4):
            r = i * 4 + k
            left, right = hc32[0, pl.ds(r, 1), :], hc32[1, pl.ds(r, 1), :]
            edge = xc[r + 1, 0:16, :].astype(F32)
            ecol[0, pl.ds(r + 1, 1), :] = jnp.concatenate([left, edge[0:1, ch:]], axis=1)
            xc[r + 1, 0:16, 0:ch] = jnp.where(tile == 0, left, edge[:, 0:ch]).astype(BF16)
            edge = xc[r + 1, cols - 16 : cols, :].astype(F32)
            ecol[1, pl.ds(r + 1, 1), :] = jnp.concatenate([edge[15:16, : 2 * ch], right], axis=1)
            xc[r + 1, cols - 16 : cols, 2 * ch :] = jnp.where(tile == 15, right, edge[:, 2 * ch :]).astype(BF16)
        return carry

    lax.fori_loop(0, rows // 4, patch, 0)
    lhs = [jnp.concatenate([xc[r + a] for a in range(3)], axis=1) for r in (0, rows - 1)]
    for side in range(2):
        lhs.append(jnp.concatenate([ecol[side, a : a + rows, :] for a in range(3)], axis=1).astype(BF16))
    cot = [c_ref[0].astype(F32), c_ref[rows - 1].astype(F32), scol32[0], scol32[1]]
    value, grad = layer(jnp.concatenate(lhs, axis=0), jnp.concatenate(cot, axis=0))
    out_ref[0] = value[0:cols].astype(BF16)
    out_ref[rows - 1] = value[cols : 2 * cols].astype(BF16)
    pg[0] = grad[0:cols].astype(BF16)
    pg[rows - 1] = grad[cols : 2 * cols].astype(BF16)
    for side in range(2):
        low = 2 * cols + side * rows
        fix[0, side] = value[low : low + rows]
        fix[1, side] = grad[low : low + rows]
        scol[1, side] = grad[low : low + rows].astype(BF16)

    def put_columns(i, carry):
        for k in range(4):
            r = i * 4 + k
            for which, ref in ((0, out_ref), (1, pg)):
                for side, start, line_at in ((0, 0, 0), (1, cols - 16, 15)):
                    old = ref[r, start : start + 16, :].astype(F32)
                    new = jnp.where(tile == line_at, fix[which, side, pl.ds(r, 1), :], old)
                    ref[r, start : start + 16, :] = new.astype(BF16)
        return carry

    lax.fori_loop(0, rows // 4, put_columns, 0)

    second = halo_copies(1, pg)
    for copy in second:
        copy.start()
    store(out_ref, out_hbm)

    def turn_over(i, carry):
        r0 = i * CHUNK
        grad = pg[pl.ds(r0, CHUNK)].reshape(CHUNK * cols, ch)
        bacc[...] += jnp.sum(grad.astype(F32), axis=0, keepdims=True)
        pgt[:, pl.ds(pl.multiple_of(r0 * cols, ch), CHUNK * cols)] = grad.T
        return carry

    lax.fori_loop(0, rows // CHUNK, turn_over, 0)

    line = lax.broadcasted_iota(jnp.int32, (EXTRA, ch), 0)

    def split(total):
        first_part = total.astype(BF16).astype(F32)
        rest = total - first_part
        second_part = rest.astype(BF16).astype(F32)
        third = rest - second_part
        rows_of = jnp.where(line == 0, first_part, jnp.where(line == 1, second_part, jnp.where(line == 2, third, 0.0)))
        return rows_of.astype(BF16)

    def size(a, count):
        return slice(0, count + EXTRA if a == 0 else count)

    sent = []

    def send(phase, a, src, dst, device):
        pltpu.make_async_remote_copy(
            src_ref=src, dst_ref=dst, send_sem=gsem.at[0, phase, a], recv_sem=gsem.at[1, phase, a],
            device_id=device, device_id_type=MESH,
        ).start()

    def wait_all(phase, a, ref):
        copy = pltpu.make_async_remote_copy(
            src_ref=ref, dst_ref=ref, send_sem=gsem.at[0, phase, a], recv_sem=gsem.at[1, phase, a],
            device_id=sibling, device_id_type=MESH,
        )
        copy.wait_recv()
        sent.append(copy)

    half_rows = chips * part

    def third(a):
        window = xc[a : a + rows].reshape(rows * cols, 3 * ch)
        grad = jnp.dot(pgt[...], window, preferred_element_type=F32)
        for b in range(3):
            block = grad[:, b * ch : (b + 1) * ch].T.astype(BF16)
            low = b * ch
            while low < (b + 1) * ch:
                q = low // half_rows
                high = min((b + 1) * ch, (q + 1) * half_rows)
                sbuf[a, q, low - q * half_rows : high - q * half_rows, :] = block[low - b * ch : high - b * ch]
                low = high
        if a == 0:
            bias_rows = split(bacc[...])
            for q in range(2):
                sbuf[0, q, half_rows : half_rows + EXTRA, :] = bias_rows
        block_size = size(a, half_rows)
        send(0, a, sbuf.at[a, 1 - core, block_size], r0.at[a, block_size], sibling)

    def plane(a):
        block_size = size(a, half_rows)
        wait_all(0, a, r0.at[a, block_size])
        total = sbuf[a, core, block_size, :].astype(F32) + r0[a, block_size, :].astype(F32)
        for q in range(chips):
            s1[a, q, 0:part, :] = total[q * part : (q + 1) * part].astype(BF16)
        if a == 0:
            bias_rows = split(jnp.sum(total[half_rows:], axis=0, keepdims=True))
            for q in range(chips):
                s1[a, q, part : part + EXTRA, :] = bias_rows
        for k in range(1, chips):
            q, device = peer1(k)
            send(1, a, s1.at[a, q, size(a, part)], r1.at[a, g1, size(a, part)], device)
        r1[a, g1, size(a, part), :] = s1[a, g1, size(a, part), :]

    def added(buffer, a, count):
        total = buffer[a, 0, size(a, part), :].astype(F32)
        for q in range(1, count):
            total = total + buffer[a, q, size(a, part), :].astype(F32)
        return total

    def along(a):
        wait_all(1, a, r1.at[a, 0 : chips - 1, size(a, part)])
        total = added(r1, a, chips)
        s2[a, 0:part, :] = total[:part].astype(BF16)
        if a == 0:
            s2[a, part : part + EXTRA, :] = split(jnp.sum(total[part:], axis=0, keepdims=True))
        for k in range(1, n2):
            send(2, a, s2.at[a, size(a, part)], r2.at[a, g2, size(a, part)], peer2(k)[1])
        r2[a, g2, size(a, part), :] = s2[a, size(a, part), :]

    scale = 1.0 / math.sqrt(rows * cols * lons * lats)

    def around(a):
        wait_all(2, a, r2.at[a, 0 : n2 - 1, size(a, part)])
        total = added(r2, a, n2)
        if a == 0:
            bg_ref[...] = jnp.sum(total[part:], axis=0, keepdims=True) * scale
            store(bg_ref, bg_hbm)
        gath[a, core, g1] = (total[:part] * scale).astype(BF16)
        for k in range(1, chips):
            send(3, a, gath.at[a, core, g1], gath.at[a, core, g1], peer1(k)[1])

    def across(a):
        wait_all(3, a, gath.at[a, core, 0 : chips - 1])
        send(4, a, gath.at[a, core], gath.at[a, core], sibling)
        wg_ref[a, core] = gath[a, core].astype(F32)

    def finish(a):
        wait_all(4, a, gath.at[a, 1 - core])
        wg_ref[a, 1 - core] = gath[a, 1 - core].astype(F32)
        store(wg_ref.at[a], wg_hbm.at[a])

    third(0)
    third(1)
    plane(0)
    third(2)
    plane(1)

    halo_wait(1)
    widen(1, pg, pc)

    def backward(i, carry):
        r0 = i * CHUNK
        grad = jnp.dot(windows(pc, r0), vt[...], preferred_element_type=F32)
        gin_ref[pl.ds(r0, CHUNK)] = grad.astype(BF16).reshape(CHUNK, cols, ch)
        return carry

    steps = rows // CHUNK
    plane(2)
    along(0)
    lax.fori_loop(0, steps // 3, backward, 0)
    along(1)
    lax.fori_loop(steps // 3, 2 * steps // 3, backward, 0)
    along(2)
    around(0)
    lax.fori_loop(2 * steps // 3, steps, backward, 0)
    around(1)
    across(0)

    def row_of(at_row, rhs):
        lhs = jnp.concatenate([pc[at_row + a] for a in range(3)], axis=1)
        gin_ref[at_row] = jnp.dot(lhs, rhs, preferred_element_type=F32).astype(BF16)

    third_of = 3 * ch
    near, far = vt[0:third_of, :], vt[2 * third_of :, :]
    row_of(0, jnp.concatenate([jnp.where(top, far, near), vt[third_of:, :]], axis=0))
    row_of(rows - 1, jnp.concatenate([vt[: 2 * third_of, :], jnp.where(bottom, near, far)], axis=0))
    store(gin_ref, gin_hbm)

    around(2)
    across(1)
    finish(0)
    across(2)
    finish(1)
    finish(2)
    for copy in first + second + sent:
        copy.wait_send()
    for copy in stores:
        copy.wait()


def store_all(*refs):
    sources, targets, staged, sems = refs[0:4], refs[4:8], refs[8:12], refs[12]
    loads = [pltpu.make_async_copy(s, v, sems.at[0, i]) for i, (s, v) in enumerate(zip(sources, staged))]
    stores = [pltpu.make_async_copy(v, t, sems.at[1, i]) for i, (v, t) in enumerate(zip(staged, targets))]
    for load in loads:
        load.start()
    for load, save in zip(loads, stores):
        load.wait()
        save.start()
    for save in stores:
        save.wait()


def shards(lons, lats, inputs, weight, bias, cotangent):
    rows, cols, ch = inputs.shape
    gl, gt = math.gcd(lons, 4), math.gcd(lats, 2)
    chips = (gl // 2) * gt
    n2 = (lons // gl) * (lats // gt)
    part = 3 * ch // (2 * chips)
    limit = 62 * 1024 * 1024
    dma = pltpu.SemaphoreType.DMA
    anywhere = pl.BlockSpec(memory_space=pltpu.HBM)
    results = pl.pallas_call(
        functools.partial(kernel, lons, lats),
        out_shape=(
            jax.ShapeDtypeStruct((rows, cols, ch), BF16),
            jax.ShapeDtypeStruct((rows, cols, ch), BF16),
            jax.ShapeDtypeStruct((3, 2, chips, part, ch), F32),
            jax.ShapeDtypeStruct((1, ch), F32),
        ),
        in_specs=[anywhere] * 4,
        out_specs=(anywhere,) * 4,
        scratch_shapes=[
            pltpu.VMEM((rows, cols, ch), BF16),
            pltpu.VMEM((3, 3, ch, ch), BF16),
            pltpu.VMEM((1, ch), F32),
            pltpu.VMEM((rows, cols, ch), BF16),
            pltpu.VMEM((rows, cols, ch), BF16),
            pltpu.VMEM((rows, cols, ch), BF16),
            pltpu.VMEM((3, 2, chips, part, ch), F32),
            pltpu.VMEM((1, ch), F32),
            pltpu.VMEM((9 * ch, ch), BF16),
            pltpu.VMEM((rows + 2, cols, 3 * ch), BF16),
            pltpu.VMEM((rows + 2, cols, 3 * ch), BF16),
            pltpu.VMEM((rows, cols, ch), BF16),
            pltpu.VMEM((ch, rows * cols), BF16),
            pltpu.VMEM((2, 2, cols, ch), BF16),
            pltpu.VMEM((2, 2, rows, ch), BF16),
            pltpu.VMEM((2, 4, 16, ch), BF16),
            pltpu.VMEM((2, rows, ch), F32),
            pltpu.VMEM((2, rows, ch), F32),
            pltpu.VMEM((2, 2, rows, ch), BF16),
            pltpu.VMEM((2, rows + 2, 3 * ch), F32),
            pltpu.VMEM((2, 2, rows, ch), F32),
            pltpu.VMEM((1, ch), F32),
            pltpu.VMEM((3, 2, chips * part + EXTRA, ch), BF16),
            pltpu.VMEM((3, chips * part + EXTRA, ch), BF16),
            pltpu.VMEM((3, chips, part + EXTRA, ch), BF16),
            pltpu.VMEM((3, chips, part + EXTRA, ch), BF16),
            pltpu.VMEM((3, part + EXTRA, ch), BF16),
            pltpu.VMEM((3, n2, part + EXTRA, ch), BF16),
            pltpu.VMEM((3, 2, chips, part, ch), BF16),
            dma((4,)),
            dma((6,)),
            dma((2, 8)),
            dma((2, 8)),
            dma((2, 5, 3)),
        ],
        compiler_params=pltpu.CompilerParams(
            collective_id=0, has_side_effects=True, vmem_limit_bytes=limit
        ),
        name="conv_silu_grads",
    )(inputs, weight, bias.reshape(1, ch), cotangent)
    outputs, input_grad, weight_grad, bias_grad = pl.pallas_call(
        store_all,
        out_shape=(
            jax.ShapeDtypeStruct((rows, cols, ch), BF16),
            jax.ShapeDtypeStruct((rows, cols, ch), BF16),
            jax.ShapeDtypeStruct((3, 2, chips, part, ch), F32),
            jax.ShapeDtypeStruct((1, ch), F32),
        ),
        in_specs=[anywhere] * 4,
        out_specs=(anywhere,) * 4,
        scratch_shapes=[
            pltpu.VMEM((rows, cols, ch), BF16),
            pltpu.VMEM((rows, cols, ch), BF16),
            pltpu.VMEM((3, 2, chips, part, ch), F32),
            pltpu.VMEM((1, ch), F32),
            dma((2, 4)),
        ],
        compiler_params=pltpu.CompilerParams(vmem_limit_bytes=limit),
        name="write_results",
    )(*results)
    return outputs, input_grad, weight_grad.reshape(3, 3, ch, ch), bias_grad.reshape(ch)


def solution(mesh):
    lons, lats = mesh.shape["lon"], mesh.shape["lat"]
    in_specs = (P("lat", "lon", None), P(), P(), P("lat", "lon", None))
    out_specs = (P("lat", "lon", None), P("lat", "lon", None), P(), P())
    return jax.shard_map(
        functools.partial(shards, lons, lats), mesh=mesh, in_specs=in_specs, out_specs=out_specs, check_vma=False
    )
```

```python
import functools
import math

import jax
import jax.numpy as jnp
from jax import lax
from jax.experimental import pallas as pl
from jax.experimental.pallas import tpu as pltpu
from jax.sharding import PartitionSpec as P

MESH = pl.DeviceIdType.MESH
F32 = jnp.float32
BF16 = jnp.bfloat16
CHUNK = 16
EXTRA = 16


def padded_cells(rows, cols, ch):
    return pl.cdiv((rows + 2) * cols, ch) * ch


def kernel(
    lons, lats, x_hbm, w_hbm, b_hbm, c_hbm,
    out_hbm, gin_hbm, wg_hbm, bg_hbm,
    x_ref, w_ref, b_ref, c_ref, out_ref, gin_ref, wg_ref, bg_ref,
    vt, xc, pc, pg, pgt, pgt3, hrows, hcols, hcorn, hc32, scol32, scol, ecol, fix, bacc,
    sbuf, r0, s1, r1, s2, r2, gath,
    lsem, osem, ssem, rsem, gsem,
):
    pairs = ((x_hbm, x_ref), (w_hbm, w_ref), (b_hbm, b_ref), (c_hbm, c_ref))
    loads = [pltpu.make_async_copy(src, dst, lsem.at[i]) for i, (src, dst) in enumerate(pairs)]
    for load in loads:
        load.start()
    rows, cols, ch = x_ref.shape
    lon, lat = lax.axis_index("lon"), lax.axis_index("lat")
    half = lons // 2
    gl, gt = math.gcd(lons, 4), math.gcd(lats, 2)
    chips = (gl // 2) * gt
    n2 = (lons // gl) * (lats // gt)
    part = 3 * ch // (2 * chips)

    top, bottom = lat == 0, lat == lats - 1
    n_lat = jnp.where(top, lat, lat - 1)
    s_lat = jnp.where(bottom, lat, lat + 1)
    n_lon = jnp.where(top, lon + half, lon)
    s_lon = jnp.where(bottom, lon + half, lon)

    def at(lon_at, lat_at):
        return (lax.rem(lon_at + lons, lons), lat_at)

    north, south = at(n_lon, n_lat), at(s_lon, s_lat)
    west, east = at(lon - 1, lat), at(lon + 1, lat)
    nw, ne = at(n_lon - 1, n_lat), at(n_lon + 1, n_lat)
    sw, se = at(s_lon - 1, s_lat), at(s_lon + 1, s_lat)

    core = lax.rem(lon, 2)
    sibling = (lon + 1 - 2 * core, lat)
    g1 = (lax.rem(lon, gl) // 2) * gt + lax.rem(lat, gt)
    g2 = (lon // gl) * (lats // gt) + lat // gt

    def peer1(k):
        q = lax.rem(g1 + k, chips)
        return q, ((lon // gl) * gl + (q // gt) * 2 + core, (lat // gt) * gt + lax.rem(q, gt))

    def peer2(k):
        q = lax.rem(g2 + k, n2)
        wide = lats // gt
        return q, ((q // wide) * gl + lax.rem(lon, gl), lax.rem(q, wide) * gt + lax.rem(lat, gt))

    barrier = pltpu.get_barrier_semaphore()
    greeted = [north, south, west, east, nw, ne, sw, se]
    greeted += [sibling] + [peer1(k)[1] for k in range(1, chips)] + [peer2(k)[1] for k in range(1, n2)]
    for device in greeted:
        pl.semaphore_signal(barrier, inc=1, device_id=device, device_id_type=MESH)

    def stage_columns(src):
        def body(i, carry):
            for k in range(4):
                r = i * 4 + k
                scol32[0, pl.ds(r, 1), :] = src[r, 0:16, :].astype(F32)[0:1]
                scol32[1, pl.ds(r, 1), :] = src[r, cols - 16 : cols, :].astype(F32)[15:16]
            return carry

        lax.fori_loop(0, rows // 4, body, 0)

    def halo_copies(turn, src):
        lo, hi = slice(0, 16), slice(cols - 16, cols)
        to_north = jnp.where(top, 0, 1)
        to_south = jnp.where(bottom, 1, 0)
        to_nw, to_ne = jnp.where(top, 1, 3), jnp.where(top, 0, 2)
        to_sw, to_se = jnp.where(bottom, 3, 1), jnp.where(bottom, 2, 0)
        plan = [
            (scol.at[turn, 1], hcols.at[turn, 0], 2, east),
            (scol.at[turn, 0], hcols.at[turn, 1], 3, west),
            (src.at[0], hrows.at[turn, to_north], to_north, north),
            (src.at[rows - 1], hrows.at[turn, to_south], to_south, south),
            (src.at[0, lo, :], hcorn.at[turn, to_nw], 4 + to_nw, nw),
            (src.at[0, hi, :], hcorn.at[turn, to_ne], 4 + to_ne, ne),
            (src.at[rows - 1, lo, :], hcorn.at[turn, to_sw], 4 + to_sw, sw),
            (src.at[rows - 1, hi, :], hcorn.at[turn, to_se], 4 + to_se, se),
        ]
        return [
            pltpu.make_async_remote_copy(
                src_ref=s, dst_ref=d, send_sem=ssem.at[turn, i], recv_sem=rsem.at[turn, sem],
                device_id=device, device_id_type=MESH,
            )
            for i, (s, d, sem, device) in enumerate(plan)
        ]

    def halo_wait(turn):
        slots = [hrows.at[turn, 0], hrows.at[turn, 1], hcols.at[turn, 0], hcols.at[turn, 1]]
        slots += [hcorn.at[turn, i] for i in range(4)]
        for i, slot in enumerate(slots):
            pltpu.make_async_remote_copy(
                src_ref=slot, dst_ref=slot, send_sem=ssem.at[turn, i], recv_sem=rsem.at[turn, i],
                device_id=east, device_id_type=MESH,
            ).wait_recv()

    place = lax.broadcasted_iota(jnp.int32, (cols, ch), 0)

    def put_row(dst, at_row, centre, west_cell, east_cell):
        wide = centre.astype(F32)
        before = jnp.where(place == 0, west_cell, pltpu.roll(wide, 1, 0))
        after = jnp.where(place == cols - 1, east_cell, pltpu.roll(wide, cols - 1, 0))
        dst[at_row, :, 0:ch] = before.astype(BF16)
        dst[at_row, :, ch : 2 * ch] = centre
        dst[at_row, :, 2 * ch : 3 * ch] = after.astype(BF16)

    def widen(turn, src, dst):
        hc32[...] = hcols[turn].astype(F32)

        def body(i, carry):
            for k in range(4):
                r = i * 4 + k
                put_row(dst, r + 1, src[r], hc32[0, pl.ds(r, 1), :], hc32[1, pl.ds(r, 1), :])
            return carry

        lax.fori_loop(0, rows // 4, body, 0)
        for side, at_row in ((0, 0), (1, rows + 1)):
            west_cell = hcorn[turn, 2 * side].astype(F32)[15:16]
            east_cell = hcorn[turn, 2 * side + 1].astype(F32)[0:1]
            put_row(dst, at_row, hrows[turn, side], west_cell, east_cell)

    def windows(src, r0):
        return jnp.concatenate(
            [src[pl.ds(r0 + a, CHUNK)].reshape(CHUNK * cols, 3 * ch) for a in range(3)], axis=1
        )

    loads[0].wait()
    stage_columns(x_ref)
    scol[0] = scol32[...].astype(BF16)
    pl.semaphore_wait(barrier, len(greeted))
    first = halo_copies(0, x_ref)
    for copy in first:
        copy.start()

    nothing = jnp.zeros((1, ch), F32)

    def widen_alone(i, carry):
        for k in range(4):
            put_row(xc, i * 4 + k + 1, x_ref[i * 4 + k], nothing, nothing)
        return carry

    lax.fori_loop(0, rows // 4, widen_alone, 0)
    xc[0] = jnp.zeros((cols, 3 * ch), BF16)
    cells = padded_cells(rows, cols, ch)
    for r in range(rows + 1, pl.cdiv(cells, cols)):
        xc[r] = jnp.zeros((cols, 3 * ch), BF16)
    bacc[...] = jnp.zeros_like(bacc)
    for load in loads[1:]:
        load.wait()
    stores = []

    def store(src, dst):
        copy = pltpu.make_async_copy(src, dst, osem.at[len(stores)])
        copy.start()
        stores.append(copy)

    def layer(lhs, cot):
        pre = jnp.dot(lhs, w_ref[...].reshape(9 * ch, ch), preferred_element_type=F32) + b_ref[...]
        sig = 0.5 * jnp.tanh(0.5 * pre) + 0.5
        return pre * sig, cot * sig * (1.0 + pre * (1.0 - sig))

    def forward(i, carry):
        r0 = i * CHUNK
        cot = c_ref[pl.ds(r0, CHUNK)].reshape(CHUNK * cols, ch).astype(F32)
        value, grad = layer(windows(xc, r0), cot)
        out_ref[pl.ds(r0, CHUNK)] = value.astype(BF16).reshape(CHUNK, cols, ch)
        pg[pl.ds(r0, CHUNK)] = grad.astype(BF16).reshape(CHUNK, cols, ch)
        return carry

    lax.fori_loop(0, rows // CHUNK, forward, 0)
    for a in range(3):
        for b in range(3):
            vt[(3 * a + b) * ch : (3 * a + b + 1) * ch, :] = w_ref[2 - a, 2 - b].T
    stage_columns(c_ref)

    halo_wait(0)
    hc32[...] = hcols[0].astype(F32)
    for side, at_row in ((0, 0), (1, rows + 1)):
        west_cell = hcorn[0, 2 * side].astype(F32)[15:16]
        east_cell = hcorn[0, 2 * side + 1].astype(F32)[0:1]
        put_row(xc, at_row, hrows[0, side], west_cell, east_cell)
        ecol[0, at_row : at_row + 1, :] = xc[at_row, 0:16, :].astype(F32)[0:1]
        ecol[1, at_row : at_row + 1, :] = xc[at_row, cols - 16 : cols, :].astype(F32)[15:16]
    tile = lax.broadcasted_iota(jnp.int32, (16, ch), 0)

    def patch(i, carry):
        for k in range(4):
            r = i * 4 + k
            left, right = hc32[0, pl.ds(r, 1), :], hc32[1, pl.ds(r, 1), :]
            edge = xc[r + 1, 0:16, :].astype(F32)
            ecol[0, pl.ds(r + 1, 1), :] = jnp.concatenate([left, edge[0:1, ch:]], axis=1)
            xc[r + 1, 0:16, 0:ch] = jnp.where(tile == 0, left, edge[:, 0:ch]).astype(BF16)
            edge = xc[r + 1, cols - 16 : cols, :].astype(F32)
            ecol[1, pl.ds(r + 1, 1), :] = jnp.concatenate([edge[15:16, : 2 * ch], right], axis=1)
            xc[r + 1, cols - 16 : cols, 2 * ch :] = jnp.where(tile == 15, right, edge[:, 2 * ch :]).astype(BF16)
        return carry

    lax.fori_loop(0, rows // 4, patch, 0)
    lhs = [jnp.concatenate([xc[r + a] for a in range(3)], axis=1) for r in (0, rows - 1)]
    for side in range(2):
        lhs.append(jnp.concatenate([ecol[side, a : a + rows, :] for a in range(3)], axis=1).astype(BF16))
    cot = [c_ref[0].astype(F32), c_ref[rows - 1].astype(F32), scol32[0], scol32[1]]
    value, grad = layer(jnp.concatenate(lhs, axis=0), jnp.concatenate(cot, axis=0))
    out_ref[0] = value[0:cols].astype(BF16)
    out_ref[rows - 1] = value[cols : 2 * cols].astype(BF16)
    pg[0] = grad[0:cols].astype(BF16)
    pg[rows - 1] = grad[cols : 2 * cols].astype(BF16)
    for side in range(2):
        low = 2 * cols + side * rows
        fix[0, side] = value[low : low + rows]
        fix[1, side] = grad[low : low + rows]
        scol[1, side] = grad[low : low + rows].astype(BF16)

    def put_columns(i, carry):
        for k in range(4):
            r = i * 4 + k
            for which, ref in ((0, out_ref), (1, pg)):
                for side, start, line_at in ((0, 0, 0), (1, cols - 16, 15)):
                    old = ref[r, start : start + 16, :].astype(F32)
                    new = jnp.where(tile == line_at, fix[which, side, pl.ds(r, 1), :], old)
                    ref[r, start : start + 16, :] = new.astype(BF16)
        return carry

    lax.fori_loop(0, rows // 4, put_columns, 0)

    second = halo_copies(1, pg)
    for copy in second:
        copy.start()
    store(out_ref, out_hbm)

    def turn_over(i, carry):
        r0 = i * CHUNK
        grad = pg[pl.ds(r0, CHUNK)].reshape(CHUNK * cols, ch)
        bacc[...] += jnp.sum(grad.astype(F32), axis=0, keepdims=True)
        pgt[:, pl.ds(pl.multiple_of(r0 * cols, ch), CHUNK * cols)] = grad.T
        return carry

    lax.fori_loop(0, rows // CHUNK, turn_over, 0)

    line = lax.broadcasted_iota(jnp.int32, (EXTRA, ch), 0)

    def split(total):
        first_part = total.astype(BF16).astype(F32)
        rest = total - first_part
        second_part = rest.astype(BF16).astype(F32)
        third = rest - second_part
        rows_of = jnp.where(line == 0, first_part, jnp.where(line == 1, second_part, jnp.where(line == 2, third, 0.0)))
        return rows_of.astype(BF16)

    def size(a, count):
        return slice(0, count + EXTRA if a == 0 else count)

    sent = []

    def send(phase, a, src, dst, device):
        pltpu.make_async_remote_copy(
            src_ref=src, dst_ref=dst, send_sem=gsem.at[0, phase, a], recv_sem=gsem.at[1, phase, a],
            device_id=device, device_id_type=MESH,
        ).start()

    def wait_all(phase, a, ref):
        copy = pltpu.make_async_remote_copy(
            src_ref=ref, dst_ref=ref, send_sem=gsem.at[0, phase, a], recv_sem=gsem.at[1, phase, a],
            device_id=sibling, device_id_type=MESH,
        )
        copy.wait_recv()
        sent.append(copy)

    half_rows = chips * part

    def third(a):
        grad = kernel_terms[a * ch : (a + 1) * ch]
        for b in range(3):
            block = grad[:, b * ch : (b + 1) * ch].T.astype(BF16)
            low = b * ch
            while low < (b + 1) * ch:
                q = low // half_rows
                high = min((b + 1) * ch, (q + 1) * half_rows)
                sbuf[a, q, low - q * half_rows : high - q * half_rows, :] = block[low - b * ch : high - b * ch]
                low = high
        if a == 0:
            bias_rows = split(bacc[...])
            for q in range(2):
                sbuf[0, q, half_rows : half_rows + EXTRA, :] = bias_rows
        block_size = size(a, half_rows)
        send(0, a, sbuf.at[a, 1 - core, block_size], r0.at[a, block_size], sibling)

    def plane(a):
        block_size = size(a, half_rows)
        wait_all(0, a, r0.at[a, block_size])
        total = sbuf[a, core, block_size, :].astype(F32) + r0[a, block_size, :].astype(F32)
        for q in range(chips):
            s1[a, q, 0:part, :] = total[q * part : (q + 1) * part].astype(BF16)
        if a == 0:
            bias_rows = split(jnp.sum(total[half_rows:], axis=0, keepdims=True))
            for q in range(chips):
                s1[a, q, part : part + EXTRA, :] = bias_rows
        for k in range(1, chips):
            q, device = peer1(k)
            send(1, a, s1.at[a, q, size(a, part)], r1.at[a, g1, size(a, part)], device)
        r1[a, g1, size(a, part), :] = s1[a, g1, size(a, part), :]

    def added(buffer, a, count):
        total = buffer[a, 0, size(a, part), :].astype(F32)
        for q in range(1, count):
            total = total + buffer[a, q, size(a, part), :].astype(F32)
        return total

    def along(a):
        wait_all(1, a, r1.at[a, 0 : chips - 1, size(a, part)])
        total = added(r1, a, chips)
        s2[a, 0:part, :] = total[:part].astype(BF16)
        if a == 0:
            s2[a, part : part + EXTRA, :] = split(jnp.sum(total[part:], axis=0, keepdims=True))
        for k in range(1, n2):
            send(2, a, s2.at[a, size(a, part)], r2.at[a, g2, size(a, part)], peer2(k)[1])
        r2[a, g2, size(a, part), :] = s2[a, size(a, part), :]

    scale = 1.0 / math.sqrt(rows * cols * lons * lats)

    def around(a):
        wait_all(2, a, r2.at[a, 0 : n2 - 1, size(a, part)])
        total = added(r2, a, n2)
        if a == 0:
            bg_ref[...] = jnp.sum(total[part:], axis=0, keepdims=True) * scale
            store(bg_ref, bg_hbm)
        gath[a, core, g1] = (total[:part] * scale).astype(BF16)
        for k in range(1, chips):
            send(3, a, gath.at[a, core, g1], gath.at[a, core, g1], peer1(k)[1])

    def across(a):
        wait_all(3, a, gath.at[a, core, 0 : chips - 1])
        send(4, a, gath.at[a, core], gath.at[a, core], sibling)
        wg_ref[a, core] = gath[a, core].astype(F32)

    def finish(a):
        wait_all(4, a, gath.at[a, 1 - core])
        wg_ref[a, 1 - core] = gath[a, 1 - core].astype(F32)
        store(wg_ref.at[a], wg_hbm.at[a])

    turned = pgt[...]
    for a in range(3):
        ends = [jnp.zeros((ch, a * cols), BF16), jnp.zeros((ch, cells - (rows + a) * cols), BF16)]
        pgt3[a * ch : (a + 1) * ch, :] = jnp.concatenate(([ends[0]] if a else []) + [turned, ends[1]], axis=1)
    held = xc[...].reshape(pl.cdiv(cells, cols) * cols, 3 * ch)[:cells]
    kernel_terms = jnp.dot(pgt3[...], held, preferred_element_type=F32)
    for a in range(3):
        third(a)

    halo_wait(1)
    widen(1, pg, pc)

    def backward(i, carry):
        r0 = i * CHUNK
        grad = jnp.dot(windows(pc, r0), vt[...], preferred_element_type=F32)
        gin_ref[pl.ds(r0, CHUNK)] = grad.astype(BF16).reshape(CHUNK, cols, ch)
        return carry

    steps = rows // CHUNK
    for a in range(3):
        plane(a)
    lax.fori_loop(0, steps // 3, backward, 0)
    along(0)
    along(1)
    along(2)
    lax.fori_loop(steps // 3, 2 * steps // 3, backward, 0)
    around(0)
    around(1)
    around(2)
    lax.fori_loop(2 * steps // 3, steps, backward, 0)
    across(0)

    def row_of(at_row, rhs):
        lhs = jnp.concatenate([pc[at_row + a] for a in range(3)], axis=1)
        gin_ref[at_row] = jnp.dot(lhs, rhs, preferred_element_type=F32).astype(BF16)

    third_of = 3 * ch
    near, far = vt[0:third_of, :], vt[2 * third_of :, :]
    row_of(0, jnp.concatenate([jnp.where(top, far, near), vt[third_of:, :]], axis=0))
    row_of(rows - 1, jnp.concatenate([vt[: 2 * third_of, :], jnp.where(bottom, near, far)], axis=0))
    store(gin_ref, gin_hbm)

    across(1)
    finish(0)
    across(2)
    finish(1)
    finish(2)
    for copy in first + second + sent:
        copy.wait_send()
    for copy in stores:
        copy.wait()


def store_all(*refs):
    sources, targets, staged, sems = refs[0:4], refs[4:8], refs[8:12], refs[12]
    loads = [pltpu.make_async_copy(s, v, sems.at[0, i]) for i, (s, v) in enumerate(zip(sources, staged))]
    stores = [pltpu.make_async_copy(v, t, sems.at[1, i]) for i, (v, t) in enumerate(zip(staged, targets))]
    for load in loads:
        load.start()
    for load, save in zip(loads, stores):
        load.wait()
        save.start()
    for save in stores:
        save.wait()


def shards(lons, lats, inputs, weight, bias, cotangent):
    rows, cols, ch = inputs.shape
    gl, gt = math.gcd(lons, 4), math.gcd(lats, 2)
    chips = (gl // 2) * gt
    n2 = (lons // gl) * (lats // gt)
    part = 3 * ch // (2 * chips)
    cells = padded_cells(rows, cols, ch)
    limit = 62 * 1024 * 1024
    dma = pltpu.SemaphoreType.DMA
    anywhere = pl.BlockSpec(memory_space=pltpu.HBM)
    results = pl.pallas_call(
        functools.partial(kernel, lons, lats),
        out_shape=(
            jax.ShapeDtypeStruct((rows, cols, ch), BF16),
            jax.ShapeDtypeStruct((rows, cols, ch), BF16),
            jax.ShapeDtypeStruct((3, 2, chips, part, ch), F32),
            jax.ShapeDtypeStruct((1, ch), F32),
        ),
        in_specs=[anywhere] * 4,
        out_specs=(anywhere,) * 4,
        scratch_shapes=[
            pltpu.VMEM((rows, cols, ch), BF16),
            pltpu.VMEM((3, 3, ch, ch), BF16),
            pltpu.VMEM((1, ch), F32),
            pltpu.VMEM((rows, cols, ch), BF16),
            pltpu.VMEM((rows, cols, ch), BF16),
            pltpu.VMEM((rows, cols, ch), BF16),
            pltpu.VMEM((3, 2, chips, part, ch), F32),
            pltpu.VMEM((1, ch), F32),
            pltpu.VMEM((9 * ch, ch), BF16),
            pltpu.VMEM((pl.cdiv(cells, cols), cols, 3 * ch), BF16),
            pltpu.VMEM((rows + 2, cols, 3 * ch), BF16),
            pltpu.VMEM((rows, cols, ch), BF16),
            pltpu.VMEM((ch, rows * cols), BF16),
            pltpu.VMEM((3 * ch, cells), BF16),
            pltpu.VMEM((2, 2, cols, ch), BF16),
            pltpu.VMEM((2, 2, rows, ch), BF16),
            pltpu.VMEM((2, 4, 16, ch), BF16),
            pltpu.VMEM((2, rows, ch), F32),
            pltpu.VMEM((2, rows, ch), F32),
            pltpu.VMEM((2, 2, rows, ch), BF16),
            pltpu.VMEM((2, rows + 2, 3 * ch), F32),
            pltpu.VMEM((2, 2, rows, ch), F32),
            pltpu.VMEM((1, ch), F32),
            pltpu.VMEM((3, 2, chips * part + EXTRA, ch), BF16),
            pltpu.VMEM((3, chips * part + EXTRA, ch), BF16),
            pltpu.VMEM((3, chips, part + EXTRA, ch), BF16),
            pltpu.VMEM((3, chips, part + EXTRA, ch), BF16),
            pltpu.VMEM((3, part + EXTRA, ch), BF16),
            pltpu.VMEM((3, n2, part + EXTRA, ch), BF16),
            pltpu.VMEM((3, 2, chips, part, ch), BF16),
            dma((4,)),
            dma((6,)),
            dma((2, 8)),
            dma((2, 8)),
            dma((2, 5, 3)),
        ],
        compiler_params=pltpu.CompilerParams(
            collective_id=0, has_side_effects=True, vmem_limit_bytes=limit
        ),
        name="conv_silu_grads",
    )(inputs, weight, bias.reshape(1, ch), cotangent)
    outputs, input_grad, weight_grad, bias_grad = pl.pallas_call(
        store_all,
        out_shape=(
            jax.ShapeDtypeStruct((rows, cols, ch), BF16),
            jax.ShapeDtypeStruct((rows, cols, ch), BF16),
            jax.ShapeDtypeStruct((3, 2, chips, part, ch), F32),
            jax.ShapeDtypeStruct((1, ch), F32),
        ),
        in_specs=[anywhere] * 4,
        out_specs=(anywhere,) * 4,
        scratch_shapes=[
            pltpu.VMEM((rows, cols, ch), BF16),
            pltpu.VMEM((rows, cols, ch), BF16),
            pltpu.VMEM((3, 2, chips, part, ch), F32),
            pltpu.VMEM((1, ch), F32),
            dma((2, 4)),
        ],
        compiler_params=pltpu.CompilerParams(vmem_limit_bytes=limit),
        name="write_results",
    )(*results)
    return outputs, input_grad, weight_grad.reshape(3, 3, ch, ch), bias_grad.reshape(ch)


def solution(mesh):
    lons, lats = mesh.shape["lon"], mesh.shape["lat"]
    in_specs = (P("lat", "lon", None), P(), P(), P("lat", "lon", None))
    out_specs = (P("lat", "lon", None), P("lat", "lon", None), P(), P())
    return jax.shard_map(
        functools.partial(shards, lons, lats), mesh=mesh, in_specs=in_specs, out_specs=out_specs, check_vma=False
    )
```

```python
import functools
import math

import jax
import jax.numpy as jnp
from jax import lax
from jax.experimental import pallas as pl
from jax.experimental.pallas import tpu as pltpu
from jax.sharding import PartitionSpec as P

MESH = pl.DeviceIdType.MESH
F32 = jnp.float32
BF16 = jnp.bfloat16
CHUNK = 16
EXTRA = 16


def padded_cells(rows, cols, ch):
    return pl.cdiv((rows + 2) * cols, ch) * ch


def kernel(
    lons, lats, x_hbm, w_hbm, b_hbm, c_hbm,
    out_hbm, gin_hbm, wg_hbm, bg_hbm,
    x_ref, w_ref, b_ref, c_ref, out_ref, gin_ref, wg_ref, bg_ref,
    vt, xc, pc, pg, pgt, pgt3, hrows, hcols, hcorn, hc32, scol32, scol, ecol, fix, bacc,
    sbuf, r0, s1, r1, s2, r2, gath,
    lsem, osem, ssem, rsem, gsem,
):
    pairs = ((x_hbm, x_ref), (w_hbm, w_ref), (b_hbm, b_ref), (c_hbm, c_ref))
    loads = [pltpu.make_async_copy(src, dst, lsem.at[i]) for i, (src, dst) in enumerate(pairs)]
    for load in loads:
        load.start()
    rows, cols, ch = x_ref.shape
    lon, lat = lax.axis_index("lon"), lax.axis_index("lat")
    half = lons // 2
    gl, gt = math.gcd(lons, 4), math.gcd(lats, 2)
    chips = (gl // 2) * gt
    n2 = (lons // gl) * (lats // gt)
    part = 3 * ch // (2 * chips)

    top, bottom = lat == 0, lat == lats - 1
    n_lat = jnp.where(top, lat, lat - 1)
    s_lat = jnp.where(bottom, lat, lat + 1)
    n_lon = jnp.where(top, lon + half, lon)
    s_lon = jnp.where(bottom, lon + half, lon)

    def at(lon_at, lat_at):
        return (lax.rem(lon_at + lons, lons), lat_at)

    north, south = at(n_lon, n_lat), at(s_lon, s_lat)
    west, east = at(lon - 1, lat), at(lon + 1, lat)
    nw, ne = at(n_lon - 1, n_lat), at(n_lon + 1, n_lat)
    sw, se = at(s_lon - 1, s_lat), at(s_lon + 1, s_lat)

    core = lax.rem(lon, 2)
    sibling = (lon + 1 - 2 * core, lat)
    g1 = (lax.rem(lon, gl) // 2) * gt + lax.rem(lat, gt)
    g2 = (lon // gl) * (lats // gt) + lat // gt

    def peer1(k):
        q = lax.rem(g1 + k, chips)
        return q, ((lon // gl) * gl + (q // gt) * 2 + core, (lat // gt) * gt + lax.rem(q, gt))

    def peer2(k):
        q = lax.rem(g2 + k, n2)
        wide = lats // gt
        return q, ((q // wide) * gl + lax.rem(lon, gl), lax.rem(q, wide) * gt + lax.rem(lat, gt))

    barrier = pltpu.get_barrier_semaphore()
    greeted = [north, south, west, east, nw, ne, sw, se]
    greeted += [sibling] + [peer1(k)[1] for k in range(1, chips)] + [peer2(k)[1] for k in range(1, n2)]
    for device in greeted:
        pl.semaphore_signal(barrier, inc=1, device_id=device, device_id_type=MESH)

    def stage_columns(src):
        def body(i, carry):
            for k in range(4):
                r = i * 4 + k
                scol32[0, pl.ds(r, 1), :] = src[r, 0:16, :].astype(F32)[0:1]
                scol32[1, pl.ds(r, 1), :] = src[r, cols - 16 : cols, :].astype(F32)[15:16]
            return carry

        lax.fori_loop(0, rows // 4, body, 0)

    def halo_copies(turn, src):
        lo, hi = slice(0, 16), slice(cols - 16, cols)
        to_north = jnp.where(top, 0, 1)
        to_south = jnp.where(bottom, 1, 0)
        to_nw, to_ne = jnp.where(top, 1, 3), jnp.where(top, 0, 2)
        to_sw, to_se = jnp.where(bottom, 3, 1), jnp.where(bottom, 2, 0)
        plan = [
            (scol.at[turn, 1], hcols.at[turn, 0], 2, east),
            (scol.at[turn, 0], hcols.at[turn, 1], 3, west),
            (src.at[0], hrows.at[turn, to_north], to_north, north),
            (src.at[rows - 1], hrows.at[turn, to_south], to_south, south),
            (src.at[0, lo, :], hcorn.at[turn, to_nw], 4 + to_nw, nw),
            (src.at[0, hi, :], hcorn.at[turn, to_ne], 4 + to_ne, ne),
            (src.at[rows - 1, lo, :], hcorn.at[turn, to_sw], 4 + to_sw, sw),
            (src.at[rows - 1, hi, :], hcorn.at[turn, to_se], 4 + to_se, se),
        ]
        return [
            pltpu.make_async_remote_copy(
                src_ref=s, dst_ref=d, send_sem=ssem.at[turn, i], recv_sem=rsem.at[turn, sem],
                device_id=device, device_id_type=MESH,
            )
            for i, (s, d, sem, device) in enumerate(plan)
        ]

    def halo_wait(turn):
        slots = [hrows.at[turn, 0], hrows.at[turn, 1], hcols.at[turn, 0], hcols.at[turn, 1]]
        slots += [hcorn.at[turn, i] for i in range(4)]
        for i, slot in enumerate(slots):
            pltpu.make_async_remote_copy(
                src_ref=slot, dst_ref=slot, send_sem=ssem.at[turn, i], recv_sem=rsem.at[turn, i],
                device_id=east, device_id_type=MESH,
            ).wait_recv()

    place = lax.broadcasted_iota(jnp.int32, (cols, ch), 0)

    def put_row(dst, at_row, centre, west_cell, east_cell):
        wide = centre.astype(F32)
        before = jnp.where(place == 0, west_cell, pltpu.roll(wide, 1, 0))
        after = jnp.where(place == cols - 1, east_cell, pltpu.roll(wide, cols - 1, 0))
        dst[at_row, :, 0:ch] = before.astype(BF16)
        dst[at_row, :, ch : 2 * ch] = centre
        dst[at_row, :, 2 * ch : 3 * ch] = after.astype(BF16)

    def widen(turn, src, dst):
        hc32[...] = hcols[turn].astype(F32)

        def body(i, carry):
            for k in range(4):
                r = i * 4 + k
                put_row(dst, r + 1, src[r], hc32[0, pl.ds(r, 1), :], hc32[1, pl.ds(r, 1), :])
            return carry

        lax.fori_loop(0, rows // 4, body, 0)
        for side, at_row in ((0, 0), (1, rows + 1)):
            west_cell = hcorn[turn, 2 * side].astype(F32)[15:16]
            east_cell = hcorn[turn, 2 * side + 1].astype(F32)[0:1]
            put_row(dst, at_row, hrows[turn, side], west_cell, east_cell)

    def windows(src, r0):
        return jnp.concatenate(
            [src[pl.ds(r0 + a, CHUNK)].reshape(CHUNK * cols, 3 * ch) for a in range(3)], axis=1
        )

    loads[0].wait()
    stage_columns(x_ref)
    scol[0] = scol32[...].astype(BF16)
    pl.semaphore_wait(barrier, len(greeted))
    first = halo_copies(0, x_ref)
    for copy in first:
        copy.start()

    nothing = jnp.zeros((1, ch), F32)

    def widen_alone(i, carry):
        for k in range(4):
            put_row(xc, i * 4 + k + 1, x_ref[i * 4 + k], nothing, nothing)
        return carry

    lax.fori_loop(0, rows // 4, widen_alone, 0)
    xc[0] = jnp.zeros((cols, 3 * ch), BF16)
    cells = padded_cells(rows, cols, ch)
    for r in range(rows + 1, pl.cdiv(cells, cols)):
        xc[r] = jnp.zeros((cols, 3 * ch), BF16)
    bacc[...] = jnp.zeros_like(bacc)
    for load in loads[1:]:
        load.wait()
    stores = []

    def store(src, dst):
        copy = pltpu.make_async_copy(src, dst, osem.at[len(stores)])
        copy.start()
        stores.append(copy)

    def layer(lhs, cot):
        pre = jnp.dot(lhs, w_ref[...].reshape(9 * ch, ch), preferred_element_type=F32) + b_ref[...]
        sig = 0.5 * jnp.tanh(0.5 * pre) + 0.5
        return pre * sig, cot * sig * (1.0 + pre * (1.0 - sig))

    def forward(i, carry):
        r0 = i * CHUNK
        cot = c_ref[pl.ds(r0, CHUNK)].reshape(CHUNK * cols, ch).astype(F32)
        value, grad = layer(windows(xc, r0), cot)
        out_ref[pl.ds(r0, CHUNK)] = value.astype(BF16).reshape(CHUNK, cols, ch)
        pg[pl.ds(r0, CHUNK)] = grad.astype(BF16).reshape(CHUNK, cols, ch)
        return carry

    lax.fori_loop(0, rows // CHUNK, forward, 0)
    for a in range(3):
        for b in range(3):
            vt[(3 * a + b) * ch : (3 * a + b + 1) * ch, :] = w_ref[2 - a, 2 - b].T
    stage_columns(c_ref)

    halo_wait(0)
    hc32[...] = hcols[0].astype(F32)
    for side, at_row in ((0, 0), (1, rows + 1)):
        west_cell = hcorn[0, 2 * side].astype(F32)[15:16]
        east_cell = hcorn[0, 2 * side + 1].astype(F32)[0:1]
        put_row(xc, at_row, hrows[0, side], west_cell, east_cell)
        ecol[0, at_row : at_row + 1, :] = xc[at_row, 0:16, :].astype(F32)[0:1]
        ecol[1, at_row : at_row + 1, :] = xc[at_row, cols - 16 : cols, :].astype(F32)[15:16]
    tile = lax.broadcasted_iota(jnp.int32, (16, ch), 0)

    def patch(i, carry):
        for k in range(4):
            r = i * 4 + k
            left, right = hc32[0, pl.ds(r, 1), :], hc32[1, pl.ds(r, 1), :]
            edge = xc[r + 1, 0:16, :].astype(F32)
            ecol[0, pl.ds(r + 1, 1), :] = jnp.concatenate([left, edge[0:1, ch:]], axis=1)
            xc[r + 1, 0:16, 0:ch] = jnp.where(tile == 0, left, edge[:, 0:ch]).astype(BF16)
            edge = xc[r + 1, cols - 16 : cols, :].astype(F32)
            ecol[1, pl.ds(r + 1, 1), :] = jnp.concatenate([edge[15:16, : 2 * ch], right], axis=1)
            xc[r + 1, cols - 16 : cols, 2 * ch :] = jnp.where(tile == 15, right, edge[:, 2 * ch :]).astype(BF16)
        return carry

    lax.fori_loop(0, rows // 4, patch, 0)
    lhs = [jnp.concatenate([xc[r + a] for a in range(3)], axis=1) for r in (0, rows - 1)]
    for side in range(2):
        lhs.append(jnp.concatenate([ecol[side, a : a + rows, :] for a in range(3)], axis=1).astype(BF16))
    cot = [c_ref[0].astype(F32), c_ref[rows - 1].astype(F32), scol32[0], scol32[1]]
    value, grad = layer(jnp.concatenate(lhs, axis=0), jnp.concatenate(cot, axis=0))
    out_ref[0] = value[0:cols].astype(BF16)
    out_ref[rows - 1] = value[cols : 2 * cols].astype(BF16)
    pg[0] = grad[0:cols].astype(BF16)
    pg[rows - 1] = grad[cols : 2 * cols].astype(BF16)
    for side in range(2):
        low = 2 * cols + side * rows
        fix[0, side] = value[low : low + rows]
        fix[1, side] = grad[low : low + rows]
        scol[1, side] = grad[low : low + rows].astype(BF16)

    def put_columns(i, carry):
        for k in range(4):
            r = i * 4 + k
            for which, ref in ((0, out_ref), (1, pg)):
                for side, start, line_at in ((0, 0, 0), (1, cols - 16, 15)):
                    old = ref[r, start : start + 16, :].astype(F32)
                    new = jnp.where(tile == line_at, fix[which, side, pl.ds(r, 1), :], old)
                    ref[r, start : start + 16, :] = new.astype(BF16)
        return carry

    lax.fori_loop(0, rows // 4, put_columns, 0)

    second = halo_copies(1, pg)
    for copy in second:
        copy.start()
    store(out_ref, out_hbm)

    def turn_over(i, carry):
        r0 = i * CHUNK
        grad = pg[pl.ds(r0, CHUNK)].reshape(CHUNK * cols, ch)
        bacc[...] += jnp.sum(grad.astype(F32), axis=0, keepdims=True)
        pgt[:, pl.ds(pl.multiple_of(r0 * cols, ch), CHUNK * cols)] = grad.T
        return carry

    lax.fori_loop(0, rows // CHUNK, turn_over, 0)

    line = lax.broadcasted_iota(jnp.int32, (EXTRA, ch), 0)

    def split(total):
        first_part = total.astype(BF16).astype(F32)
        rest = total - first_part
        second_part = rest.astype(BF16).astype(F32)
        third = rest - second_part
        rows_of = jnp.where(line == 0, first_part, jnp.where(line == 1, second_part, jnp.where(line == 2, third, 0.0)))
        return rows_of.astype(BF16)

    def size(a, count):
        return slice(0, count + EXTRA if a == 0 else count)

    sent = []

    def send(phase, a, src, dst, device):
        pltpu.make_async_remote_copy(
            src_ref=src, dst_ref=dst, send_sem=gsem.at[0, phase, a], recv_sem=gsem.at[1, phase, a],
            device_id=device, device_id_type=MESH,
        ).start()

    def wait_all(phase, a, ref):
        copy = pltpu.make_async_remote_copy(
            src_ref=ref, dst_ref=ref, send_sem=gsem.at[0, phase, a], recv_sem=gsem.at[1, phase, a],
            device_id=sibling, device_id_type=MESH,
        )
        copy.wait_recv()
        sent.append(copy)

    half_rows = chips * part

    def third(a, grad):
        for b in range(3):
            block = grad[b * ch : (b + 1) * ch].T.astype(BF16)
            low = b * ch
            while low < (b + 1) * ch:
                q = low // half_rows
                high = min((b + 1) * ch, (q + 1) * half_rows)
                sbuf[a, q, low - q * half_rows : high - q * half_rows, :] = block[low - b * ch : high - b * ch]
                low = high
        if a == 0:
            bias_rows = split(bacc[...])
            for q in range(2):
                sbuf[0, q, half_rows : half_rows + EXTRA, :] = bias_rows
        block_size = size(a, half_rows)
        send(0, a, sbuf.at[a, 1 - core, block_size], r0.at[a, block_size], sibling)

    def plane(a):
        block_size = size(a, half_rows)
        wait_all(0, a, r0.at[a, block_size])
        total = sbuf[a, core, block_size, :].astype(F32) + r0[a, block_size, :].astype(F32)
        for q in range(chips):
            s1[a, q, 0:part, :] = total[q * part : (q + 1) * part].astype(BF16)
        if a == 0:
            bias_rows = split(jnp.sum(total[half_rows:], axis=0, keepdims=True))
            for q in range(chips):
                s1[a, q, part : part + EXTRA, :] = bias_rows
        for k in range(1, chips):
            q, device = peer1(k)
            send(1, a, s1.at[a, q, size(a, part)], r1.at[a, g1, size(a, part)], device)
        r1[a, g1, size(a, part), :] = s1[a, g1, size(a, part), :]

    def added(buffer, a, count):
        total = buffer[a, 0, size(a, part), :].astype(F32)
        for q in range(1, count):
            total = total + buffer[a, q, size(a, part), :].astype(F32)
        return total

    def along(a):
        wait_all(1, a, r1.at[a, 0 : chips - 1, size(a, part)])
        total = added(r1, a, chips)
        s2[a, 0:part, :] = total[:part].astype(BF16)
        if a == 0:
            s2[a, part : part + EXTRA, :] = split(jnp.sum(total[part:], axis=0, keepdims=True))
        for k in range(1, n2):
            send(2, a, s2.at[a, size(a, part)], r2.at[a, g2, size(a, part)], peer2(k)[1])
        r2[a, g2, size(a, part), :] = s2[a, size(a, part), :]

    scale = 1.0 / math.sqrt(rows * cols * lons * lats)

    def around(a):
        wait_all(2, a, r2.at[a, 0 : n2 - 1, size(a, part)])
        total = added(r2, a, n2)
        if a == 0:
            bg_ref[...] = jnp.sum(total[part:], axis=0, keepdims=True) * scale
            store(bg_ref, bg_hbm)
        gath[a, core, g1] = (total[:part] * scale).astype(BF16)
        for k in range(1, chips):
            send(3, a, gath.at[a, core, g1], gath.at[a, core, g1], peer1(k)[1])

    def across(a):
        wait_all(3, a, gath.at[a, core, 0 : chips - 1])
        send(4, a, gath.at[a, core], gath.at[a, core], sibling)

    def finish(a):
        wait_all(4, a, gath.at[a, 1 - core])
        block = gath[a].reshape(3 * ch, ch).astype(F32)
        for tap in range(3):
            wg_ref[tap, a] = block[tap * ch : (tap + 1) * ch]
        store(wg_ref.at[:, a], wg_hbm.at[:, a])

    turned = pgt[...]
    for a in range(3):
        ends = [jnp.zeros((ch, a * cols), BF16), jnp.zeros((ch, cells - (rows + a) * cols), BF16)]
        pgt3[a * ch : (a + 1) * ch, :] = jnp.concatenate(([ends[0]] if a else []) + [turned, ends[1]], axis=1)
    held = xc[...].reshape(pl.cdiv(cells, cols) * cols, 3 * ch)[:cells]
    kernel_terms = jnp.dot(pgt3[...], held[:, : 2 * ch], preferred_element_type=F32)
    third(0, kernel_terms[:, :ch])
    third(1, kernel_terms[:, ch:])
    third(2, jnp.dot(pgt3[...], held[:, 2 * ch :], preferred_element_type=F32))
    plane(0)
    plane(1)

    halo_wait(1)
    widen(1, pg, pc)

    def backward(i, carry):
        r0 = i * CHUNK
        grad = jnp.dot(windows(pc, r0), vt[...], preferred_element_type=F32)
        gin_ref[pl.ds(r0, CHUNK)] = grad.astype(BF16).reshape(CHUNK, cols, ch)
        return carry

    steps = rows // CHUNK
    plane(2)
    lax.fori_loop(0, steps // 3, backward, 0)
    along(0)
    along(1)
    along(2)
    lax.fori_loop(steps // 3, 2 * steps // 3, backward, 0)
    around(0)
    around(1)
    around(2)
    lax.fori_loop(2 * steps // 3, steps, backward, 0)
    across(0)

    def row_of(at_row, rhs):
        lhs = jnp.concatenate([pc[at_row + a] for a in range(3)], axis=1)
        gin_ref[at_row] = jnp.dot(lhs, rhs, preferred_element_type=F32).astype(BF16)

    third_of = 3 * ch
    near, far = vt[0:third_of, :], vt[2 * third_of :, :]
    row_of(0, jnp.concatenate([jnp.where(top, far, near), vt[third_of:, :]], axis=0))
    row_of(rows - 1, jnp.concatenate([vt[: 2 * third_of, :], jnp.where(bottom, near, far)], axis=0))
    store(gin_ref, gin_hbm)

    across(1)
    finish(0)
    across(2)
    finish(1)
    finish(2)
    for copy in first + second + sent:
        copy.wait_send()
    for copy in stores:
        copy.wait()


def store_all(*refs):
    sources, targets, staged, sems = refs[0:4], refs[4:8], refs[8:12], refs[12]
    loads = [pltpu.make_async_copy(s, v, sems.at[0, i]) for i, (s, v) in enumerate(zip(sources, staged))]
    stores = [pltpu.make_async_copy(v, t, sems.at[1, i]) for i, (v, t) in enumerate(zip(staged, targets))]
    for load in loads:
        load.start()
    for load, save in zip(loads, stores):
        load.wait()
        save.start()
    for save in stores:
        save.wait()


def shards(lons, lats, inputs, weight, bias, cotangent):
    rows, cols, ch = inputs.shape
    gl, gt = math.gcd(lons, 4), math.gcd(lats, 2)
    chips = (gl // 2) * gt
    n2 = (lons // gl) * (lats // gt)
    part = 3 * ch // (2 * chips)
    cells = padded_cells(rows, cols, ch)
    limit = 62 * 1024 * 1024
    dma = pltpu.SemaphoreType.DMA
    anywhere = pl.BlockSpec(memory_space=pltpu.HBM)
    results = pl.pallas_call(
        functools.partial(kernel, lons, lats),
        out_shape=(
            jax.ShapeDtypeStruct((rows, cols, ch), BF16),
            jax.ShapeDtypeStruct((rows, cols, ch), BF16),
            jax.ShapeDtypeStruct((3, 3, ch, ch), F32),
            jax.ShapeDtypeStruct((1, ch), F32),
        ),
        in_specs=[anywhere] * 4,
        out_specs=(anywhere,) * 4,
        scratch_shapes=[
            pltpu.VMEM((rows, cols, ch), BF16),
            pltpu.VMEM((3, 3, ch, ch), BF16),
            pltpu.VMEM((1, ch), F32),
            pltpu.VMEM((rows, cols, ch), BF16),
            pltpu.VMEM((rows, cols, ch), BF16),
            pltpu.VMEM((rows, cols, ch), BF16),
            pltpu.VMEM((3, 3, ch, ch), F32),
            pltpu.VMEM((1, ch), F32),
            pltpu.VMEM((9 * ch, ch), BF16),
            pltpu.VMEM((pl.cdiv(cells, cols), cols, 3 * ch), BF16),
            pltpu.VMEM((rows + 2, cols, 3 * ch), BF16),
            pltpu.VMEM((rows, cols, ch), BF16),
            pltpu.VMEM((ch, rows * cols), BF16),
            pltpu.VMEM((3 * ch, cells), BF16),
            pltpu.VMEM((2, 2, cols, ch), BF16),
            pltpu.VMEM((2, 2, rows, ch), BF16),
            pltpu.VMEM((2, 4, 16, ch), BF16),
            pltpu.VMEM((2, rows, ch), F32),
            pltpu.VMEM((2, rows, ch), F32),
            pltpu.VMEM((2, 2, rows, ch), BF16),
            pltpu.VMEM((2, rows + 2, 3 * ch), F32),
            pltpu.VMEM((2, 2, rows, ch), F32),
            pltpu.VMEM((1, ch), F32),
            pltpu.VMEM((3, 2, chips * part + EXTRA, ch), BF16),
            pltpu.VMEM((3, chips * part + EXTRA, ch), BF16),
            pltpu.VMEM((3, chips, part + EXTRA, ch), BF16),
            pltpu.VMEM((3, chips, part + EXTRA, ch), BF16),
            pltpu.VMEM((3, part + EXTRA, ch), BF16),
            pltpu.VMEM((3, n2, part + EXTRA, ch), BF16),
            pltpu.VMEM((3, 2, chips, part, ch), BF16),
            dma((4,)),
            dma((6,)),
            dma((2, 8)),
            dma((2, 8)),
            dma((2, 5, 3)),
        ],
        compiler_params=pltpu.CompilerParams(
            collective_id=0, has_side_effects=True, vmem_limit_bytes=limit
        ),
        name="conv_silu_grads",
    )(inputs, weight, bias.reshape(1, ch), cotangent)
    outputs, input_grad, weight_grad, bias_grad = pl.pallas_call(
        store_all,
        out_shape=(
            jax.ShapeDtypeStruct((rows, cols, ch), BF16),
            jax.ShapeDtypeStruct((rows, cols, ch), BF16),
            jax.ShapeDtypeStruct((3, 3, ch, ch), F32),
            jax.ShapeDtypeStruct((1, ch), F32),
        ),
        in_specs=[anywhere] * 4,
        out_specs=(anywhere,) * 4,
        scratch_shapes=[
            pltpu.VMEM((rows, cols, ch), BF16),
            pltpu.VMEM((rows, cols, ch), BF16),
            pltpu.VMEM((3, 3, ch, ch), F32),
            pltpu.VMEM((1, ch), F32),
            dma((2, 4)),
        ],
        compiler_params=pltpu.CompilerParams(vmem_limit_bytes=limit),
        name="write_results",
    )(*results)
    return outputs, input_grad, weight_grad, bias_grad.reshape(ch)


def solution(mesh):
    lons, lats = mesh.shape["lon"], mesh.shape["lat"]
    in_specs = (P("lat", "lon", None), P(), P(), P("lat", "lon", None))
    out_specs = (P("lat", "lon", None), P("lat", "lon", None), P(), P())
    return jax.shard_map(
        functools.partial(shards, lons, lats), mesh=mesh, in_specs=in_specs, out_specs=out_specs, check_vma=False
    )
```
